32 devices in a mesh: gx: 8 (over y, x, core), gy: 4 (over z).
Axes of the slice: x: 2, y: 2, z: 4, core: 2. Of those that a mesh axis runs over, the one named last changes fastest.
Arguments:
- velocity: float32 [3, 512, 128, 128], P(None, 'gx', 'gy'), may hold values from -6 to 6
- inflow: float32 [3, 128, 128], P(None, 'gy'), may hold values from -6 to 6
- azimuth: float32 [32], replicated, may hold values from -3.140625 to 3.140625
- positions: int32 [32, 2], replicated, may hold values from 0 to 511, as said below
- crossings: int32 [32, 6], replicated, may hold values from -1 to 95, as said below
- lag_state: float32 [96, 128], P(('gx', 'gy')), may hold values from -0.5 to 1.5
- lag_rate: float32 [96, 128], P(('gx', 'gy')), may hold values from 0.05 to 0.8
- chord_len: float32 [128], replicated, may hold values from 0.3 to 1.5
- twist_angle: float32 [128], replicated, may hold values from -0.4 to 0.4
Outputs:
- velocity_out: float32 [3, 512, 128, 128], P(None, 'gx', 'gy')
- state_out: float32 [96, 128], P(('gx', 'gy'))
The draws below stay inside these ranges and needn't reach their ends.
Inputs may be any that keep to these rules, and one draw needn't show every extreme that they name: `positions`: every rotor's hub lies in the tile of its cell, 2 or more cells from both x edges of that tile and at most 15 cells below its upper y edge; a tile holds at most two hubs, and two hubs in one tile differ in x. `crossings`: row t lists the blades 3 r, 3 r + 1, 3 r + 2 of every rotor r whose hub lies in tile t, then of some of the rotors whose hub lies in the tile just before t along y (cyclic, same x), and -1 in the remaining entries at the end. Every blade appears in one or two rows; some rows hold 6 blades.
All inputs are finite; a program needn't handle non-finite values.
Results may differ from the reference program's by a relative error of at most 0.0003.
Values sent between devices are 32-bit elements; how exact they have to be, the bound alone decides.
A program may use at most 128 MiB of HBM per device.

```python
import math
import jax
import jax.numpy as jnp
from jax import lax

CX = 64
CY = 32
NZ = 128
SEC = 128
RADIUS = 12
HUB = 15
STEPS = 2
CAP = 6
NX = 512
NY = 128
ROTORS = 32
BLADES = 96


def farm_layout(key):
    key = jax.random.fold_in(key, 11)
    k_rot, k_perm, k_x, k_y, k_keep = jax.random.split(key, 5)
    tiles_x = NX // CX
    tiles_y = NY // CY
    tile_total = tiles_x * tiles_y
    pattern_base = jnp.array([2, 0, 2, 0], dtype=jnp.int32)
    pattern = jnp.tile(pattern_base, tiles_y // 4)
    shift_by = jax.random.randint(k_rot, (tiles_x, 1), 0, tiles_y)
    columns = (jnp.arange(tiles_y, dtype=jnp.int32)[None, :] + shift_by) % tiles_y
    tile_counts = pattern[columns].reshape(-1)
    staggered = (columns % 4 == 2).astype(jnp.int32).reshape(-1)
    slot_ends = jnp.cumsum(tile_counts)
    starts = slot_ends - tile_counts
    slot_ids = jnp.arange(ROTORS, dtype=jnp.int32)
    tile_of = jnp.sum((slot_ends[None, :] <= slot_ids[:, None]).astype(jnp.int32), axis=1)
    within = slot_ids - starts[tile_of]
    col_x = tile_of // tiles_y
    row_y = tile_of % tiles_y
    spacing = (CX - 4) // 2
    stagger = (CX - 4) // 4 if CX >= 32 else 0
    jitter_top = max(CX // 32, 2)
    jit_x = jax.random.randint(k_x, (tile_total,), 0, jitter_top)
    jit_y = jax.random.randint(k_y, (ROTORS,), 0, RADIUS + 3)
    hub_x = col_x * CX + 2 + within * spacing + stagger * staggered[tile_of] + jit_x[tile_of]
    hub_y = row_y * CY + CY - RADIUS - 3 + jit_y
    shuffle = jax.random.permutation(k_perm, ROTORS).astype(jnp.int32)
    positions = jnp.zeros((ROTORS, 2), jnp.int32).at[shuffle].set(jnp.stack([hub_x, hub_y], axis=1))
    keep_slot = jax.random.randint(k_keep, (ROTORS,), 0, 2)
    below_row = (jnp.arange(tiles_y, dtype=jnp.int32) - 1) % tiles_y
    below_tile = (jnp.arange(tiles_x, dtype=jnp.int32)[:, None] * tiles_y + below_row[None, :]).reshape(-1)
    pair_index = jnp.arange(2, dtype=jnp.int32)[None, :]
    own_valid = pair_index < tile_counts[:, None]
    own_slot = jnp.clip(starts[:, None] + pair_index, 0, ROTORS - 1)
    low_slot = jnp.clip(starts[below_tile][:, None] + pair_index, 0, ROTORS - 1)
    low_valid = (pair_index < tile_counts[below_tile][:, None]) & (keep_slot[low_slot] == 1)
    cand_slot = jnp.concatenate([own_slot, low_slot], axis=1)
    cand_valid = jnp.concatenate([own_valid, low_valid], axis=1).astype(jnp.int32)
    cand_rank = jnp.cumsum(cand_valid, axis=1) - 1
    places = jnp.arange(CAP // 3, dtype=jnp.int32)
    matches = (cand_valid[:, :, None] == 1) & (cand_rank[:, :, None] == places[None, None, :])
    picked_slot = jnp.sum(jnp.where(matches, cand_slot[:, :, None], 0), axis=1)
    picked_valid = jnp.any(matches, axis=1)
    rotor_pick = shuffle[picked_slot]
    blades = 3 * rotor_pick[:, :, None] + jnp.arange(3, dtype=jnp.int32)[None, None, :]
    listing = jnp.where(picked_valid[:, :, None], blades, -1).reshape(tile_total, CAP)
    return (positions, listing)


def draw_positions(key, part):
    return farm_layout(key)[0]


def draw_crossings(key, part):
    return farm_layout(key)[1]


def levels(own_key, dims, pieces, low, largest):
    def one(axis_at, blocks):
        steps = jax.random.uniform(jax.random.fold_in(jax.random.fold_in(own_key, 6), axis_at), (blocks,), jnp.float32, low / len(pieces), largest / len(pieces))
        return jnp.repeat(jnp.exp(steps), dims[axis_at] // blocks).reshape((-1,) + (1,) * (len(dims) - axis_at - 1))

    gain = one(*pieces[0])
    for cut in pieces[1:]:
        gain = gain * one(*cut)
    return gain


def normal_values(rng, dims, scale, most, shards=(), kind=jnp.bfloat16):
    level = levels(rng, dims, shards, -0.22, 0.18) if shards else 1.0
    entries = jax.random.normal(rng, dims, jnp.float32) * scale * level
    return jnp.minimum(jnp.maximum(entries, -most), most).astype(kind)


def setup_inputs(seed: int = 0) -> dict:
    key_list = jax.random.split(jax.random.key(seed), 10)
    velocity = normal_values(key_list[0], (3, NX, NY, NZ), 1.0, 6.0, ((1, 8), (2, 4)), jnp.float32)
    inflow = normal_values(key_list[1], (3, NY, NZ), 1.0, 6.0, ((1, 4),), jnp.float32)
    azimuth = jnp.clip(jax.random.uniform(key_list[2], (ROTORS,), jnp.float32, -3.140625, 3.140625), -3.140625, 3.140625)
    positions = draw_positions(jax.random.fold_in(key_list[9], 71), 0)
    crossings = draw_crossings(jax.random.fold_in(key_list[9], 71), 0)
    lag_state = jnp.clip(-0.5 + 2.0 * jax.random.uniform(key_list[5], (BLADES, SEC), jnp.float32) ** levels(key_list[5], (BLADES, SEC), ((0, 32),), -0.2, 0.2), -0.5, 1.5)
    lag_rate = jnp.clip(jnp.exp(math.log(0.8) - 2.7725887 * jax.random.uniform(key_list[6], (BLADES, SEC), jnp.float32) ** levels(key_list[6], (BLADES, SEC), ((0, 32),), -0.2, 0.2)), 0.05, 0.8)
    chord_len = jnp.clip(jnp.exp(jax.random.uniform(key_list[7], (SEC,), jnp.float32, math.log(0.3), math.log(1.5))), 0.3, 1.5)
    twist_angle = jnp.clip(jax.random.uniform(key_list[8], (SEC,), jnp.float32, -0.4, 0.4), -0.4, 0.4)
    return {"velocity": velocity, "inflow": inflow, "azimuth": azimuth, "positions": positions, "crossings": crossings, "lag_state": lag_state, "lag_rate": lag_rate, "chord_len": chord_len, "twist_angle": twist_angle}


EPSILON = 2.0
SUPPORT = 3.0
TURN_RATE = 0.1
SPIN = 0.25
LIFT_SLOPE = 2.0 * math.pi
FORCE_SCALE = 0.15
ADVECT = 0.5
DIFFUSE = 0.05
PRECISE = lax.Precision.HIGHEST

def taper_kernel(distance):
    square = distance * distance
    taper_term = jnp.maximum(1.0 - square / (SUPPORT * SUPPORT), 0.0)
    return jnp.exp(-square / (EPSILON * EPSILON)) * taper_term * taper_term / (EPSILON * math.sqrt(math.pi))

def blade_geometry(blade_ids, azimuth, step_id, sections):
    rotor_ids = blade_ids // 3
    azimuths = azimuth[rotor_ids] + TURN_RATE * step_id + 2.0 * math.pi / 3.0 * (blade_ids % 3).astype(jnp.float32)
    radius = RADIUS * (jnp.arange(sections, dtype=jnp.float32) + 0.5) / sections
    return (jnp.cos(azimuths), jnp.sin(azimuths), radius)

def window_kernels(cosines, sine_az, radius, depth_z):
    offsets_y = jnp.arange(2 * RADIUS + 7, dtype=jnp.float32) - (RADIUS + 3)
    heights = jnp.arange(depth_z, dtype=jnp.float32)
    kern_y = taper_kernel(offsets_y[None, None, :] - radius[None, :, None] * sine_az[:, None, None])
    kern_z = taper_kernel(heights[None, None, :] - HUB - radius[None, :, None] * cosines[:, None, None])
    return (kern_y, kern_z)

def blade_forces(samples, lag_now, rates, cosines, sine_az, radius, chord_len, twist_angle):
    cos_b = cosines[:, None]
    sin_b = sine_az[:, None]
    axial_wind = samples[:, 0]
    tangential = SPIN * radius[None, :] - (samples[:, 1] * cos_b - samples[:, 2] * sin_b)
    magnitude = jnp.sqrt(axial_wind * axial_wind + tangential * tangential + 1.0)
    lift_static = LIFT_SLOPE * (axial_wind * jnp.cos(twist_angle) - tangential * jnp.sin(twist_angle)) / magnitude
    updated = lag_now + rates * (lift_static - lag_now)
    lift_force = FORCE_SCALE * chord_len * updated * magnitude
    forces = jnp.stack([-lift_force * tangential, lift_force * axial_wind * cos_b, -lift_force * axial_wind * sin_b], axis=1)
    return (updated, forces)

def advance(velocity, inflow, body_force):

    def advance_one(operands):
        grid_part, inflow_edge, push_part = operands
        x_prev = jnp.concatenate([inflow_edge[None], grid_part[:-1]], axis=0)
        x_next = jnp.concatenate([grid_part[1:], grid_part[-1:]], axis=0)
        y_next = jnp.roll(grid_part, -1, axis=1)
        y_prev = jnp.roll(grid_part, 1, axis=1)
        z_next = jnp.concatenate([grid_part[:, :, 1:], grid_part[:, :, -1:]], axis=2)
        z_prev = jnp.concatenate([jnp.zeros_like(grid_part[:, :, :1]), grid_part[:, :, :-1]], axis=2)
        neighbours = x_prev + x_next + y_next + y_prev + z_next + z_prev
        return grid_part + ADVECT * (x_prev - grid_part) + DIFFUSE * (neighbours - 6.0 * grid_part) + push_part
    return lax.map(advance_one, (velocity, inflow, body_force))

def reference(velocity, inflow, azimuth, positions, crossings, lag_state, lag_rate, chord_len, twist_angle):
    blade_ids = jnp.arange(BLADES, dtype=jnp.int32)
    rotor_ids = blade_ids // 3
    hub_x = positions[rotor_ids, 0]
    hub_y = positions[rotor_ids, 1]
    member = jnp.any(crossings[:, :, None] == blade_ids[None, None, :], axis=1).astype(jnp.float32)
    reach_y = RADIUS + 3
    offsets_x = jnp.arange(5, dtype=jnp.int32) - 2
    offsets_y = jnp.arange(2 * reach_y + 1, dtype=jnp.int32) - reach_y
    kern_x = taper_kernel(offsets_x.astype(jnp.float32))
    lag_now = lag_state
    for step_id in range(STEPS):
        cosines, sine_az, radius = blade_geometry(blade_ids, azimuth, step_id, SEC)
        kern_y, kern_z = window_kernels(cosines, sine_az, radius, NZ)

        def locate(blade_id):
            cells_x = hub_x[blade_id] + offsets_x
            cells_y = (hub_y[blade_id] + offsets_y) % NY
            tile_ids = hub_x[blade_id] // CX * (NY // CY) + cells_y // CY
            return (cells_x, cells_y, member[tile_ids, blade_id])

        def sample_one(blade_id):
            cells_x, cells_y, member_mask = locate(blade_id)
            window = velocity[:, cells_x[:, None], cells_y[None, :], :]
            flattened = jnp.einsum('i,cijz->cjz', kern_x, window, precision=PRECISE) * member_mask[None, :, None]
            inner_sum = jnp.dot(flattened.reshape(-1, NZ), kern_z[blade_id].T, precision=PRECISE).reshape(3, -1, SEC)
            return lax.optimization_barrier(jnp.sum(inner_sum * kern_y[blade_id].T[None], axis=1))
        samples = lax.map(sample_one, blade_ids)
        lag_now, forces = blade_forces(samples, lag_now, lag_rate, cosines, sine_az, radius, chord_len, twist_angle)

        def spread_one(force_field, blade_id):
            cells_x, cells_y, member_mask = locate(blade_id)
            weighted = forces[blade_id][:, None, :] * kern_y[blade_id].T[None]
            spread = jnp.dot(weighted.reshape(-1, SEC), kern_z[blade_id], precision=PRECISE).reshape(3, -1, NZ)
            spread = spread * member_mask[None, :, None]
            block_add = kern_x[None, :, None, None] * spread[:, None]
            return (force_field.at[:, cells_x[:, None], cells_y[None, :], :].add(block_add), None)
        body_force, _ = lax.scan(spread_one, jnp.zeros_like(velocity), blade_ids)
        velocity = advance(velocity, inflow, body_force)
    return (velocity, lag_now)
```

```python
import functools
import math

import jax
import jax.numpy as jnp
from jax import lax
from jax.experimental import pallas as pl
from jax.experimental.pallas import tpu as pltpu
from jax.sharding import PartitionSpec as P

RADIUS = 12
HUB = 15
STEPS = 2
EPSILON = 2.0
SUPPORT = 3.0
TURN_RATE = 0.1
SPIN = 0.25
LIFT_SLOPE = 2.0 * math.pi
FORCE_SCALE = 0.15
ADVECT = 0.5
DIFFUSE = 0.05
PRECISE = lax.Precision.HIGH
MESH = pl.DeviceIdType.MESH
BLADES = 3
ENTRIES = 2
ROWS = 8
UNROLL = 4
SLAB = 8
CHUNKS = 4


def taper_const(distance):
    square = distance * distance
    term = max(1.0 - square / (SUPPORT * SUPPORT), 0.0)
    return math.exp(-square / EPSILON**2) * term * term / (EPSILON * math.sqrt(math.pi))


KERN_X = [taper_const(float(i)) for i in range(3)]


def taper_kernel(distance):
    square = distance * distance
    term = jnp.maximum(1.0 - square * (1.0 / (SUPPORT * SUPPORT)), 0.0)
    return (
        jnp.exp(square * (-1.0 / (EPSILON * EPSILON)))
        * (term * term)
        * (1.0 / (EPSILON * math.sqrt(math.pi)))
    )


def weight_x(offset):
    dist = jnp.abs(offset)
    return jnp.where(
        dist == 0,
        KERN_X[0],
        jnp.where(dist == 1, KERN_X[1], jnp.where(dist == 2, KERN_X[2], 0.0)),
    ).astype(jnp.float32)


def farm_kernel(
    nx,
    ny,
    vel_hbm,
    inflow_hbm,
    az_hbm,
    pos_hbm,
    cross_hbm,
    lag_hbm,
    rate_hbm,
    chord_hbm,
    twist_hbm,
    out_ref,
    state_ref,
    inflow_ref,
    az_ref,
    pos_ref,
    cross_ref,
    lag_ref,
    rate_ref,
    chord_ref,
    twist_ref,
    grid0,
    grid1,
    halo_x,
    halo_y,
    face_y,
    part_out,
    part_in,
    kern_y,
    kern_z,
    spread,
    lag_pack,
    lag_in,
    home_out,
    home_in,
    small_sem,
    load_sem,
    hx_send,
    hx_recv,
    hy_send,
    hy_recv,
    ps_send,
    ps_recv,
    lag_send,
    lag_recv,
    home_send,
    home_recv,
):
    f32 = jnp.float32
    _, cx, cy, nz = grid0.shape
    total_y = cy * ny
    devices = nx * ny
    gx = lax.axis_index("gx")
    gy = lax.axis_index("gy")
    tile = gx * ny + gy
    up = lax.rem(gy + 1, ny)
    down = lax.rem(gy + ny - 1, ny)

    def peer(d):
        other = lax.rem(tile + d, devices)
        return (other // ny, lax.rem(other, ny))

    smalls = [
        pltpu.make_async_copy(source, target, small_sem.at[i])
        for i, (source, target) in enumerate(
            (
                (az_hbm, az_ref),
                (pos_hbm, pos_ref),
                (cross_hbm, cross_ref),
                (lag_hbm, lag_ref),
                (rate_hbm, rate_ref),
                (chord_hbm, chord_ref),
                (twist_hbm, twist_ref),
                (inflow_hbm, inflow_ref),
            )
        )
    ]
    for copy in smalls:
        copy.start()
    slabs = [
        pltpu.make_async_copy(vel_hbm.at[:, :, rows], grid0.at[:, :, rows], load_sem.at[i])
        for i, rows in enumerate((pl.ds(cy - SLAB, SLAB), pl.ds(0, SLAB), pl.ds(SLAB, cy - 2 * SLAB)))
    ]
    for copy in slabs:
        copy.start()

    barrier = pltpu.get_barrier_semaphore()

    def greet(d, carry):
        pl.semaphore_signal(barrier, inc=1, device_id=peer(d), device_id_type=MESH)
        return carry

    lax.fori_loop(1, devices, greet, 0)

    for copy in smalls:
        copy.wait()

    rotor, hub_x, load_x, shift_y, valid, az = [], [], [], [], [], []
    for e in range(ENTRIES):
        blade = cross_ref[BLADES * e, tile]
        r = jnp.where(blade >= 0, blade, 0) // BLADES
        rotor.append(jnp.where(blade >= 0, r, -1))
        valid.append(jnp.where(blade >= 0, 1.0, 0.0).astype(f32))
        hub_x.append(jnp.where(blade >= 0, pos_ref[0, r] - gx * cx, 2))
        load_x.append(jnp.clip(hub_x[e], 2, cx - 3))
        off = gy * cy - pos_ref[1, r] + total_y + total_y // 2
        shift_y.append(lax.rem(off, total_y) - total_y // 2)
        az.append(az_ref[r])

    listed = [[cross_ref[BLADES * f, gx * ny + k] for f in range(ENTRIES)] for k in range(ny)]

    def matches(other):
        found = []
        for f in range(ENTRIES):
            blade = cross_ref[BLADES * f, other]
            found.append(jnp.where(blade >= 0, jnp.where(blade >= 0, blade, 0) // BLADES, -2))
        return [
            [jnp.where(rotor[e] == found[f], 1.0, 0.0).astype(f32) for f in range(ENTRIES)]
            for e in range(ENTRIES)
        ]

    row = lax.broadcasted_iota(jnp.int32, (ROWS, nz), 0)
    first = row < BLADES
    lane8 = lax.broadcasted_iota(jnp.int32, (ROWS, nz), 1).astype(f32)
    radius = RADIUS * (lane8 + 0.5) / nz
    spin = jnp.where(first, row, row - BLADES).astype(f32) * (2.0 * math.pi / 3.0)
    base = jnp.where(first, az[0], az[1])
    mask_rows = []
    for other in (gx * ny + down, gx * ny + up):
        m = matches(other)
        mask_rows.append(
            (jnp.where(first, m[0][0], m[1][1]), jnp.where(first, m[0][1], m[1][0]))
        )
    cos_all, sin_all = [], []
    rows_y = lax.broadcasted_iota(jnp.int32, (cy, nz), 0)
    rows_z = lax.broadcasted_iota(jnp.int32, (nz, nz), 0).astype(f32) - HUB
    for n in range(STEPS):
        theta = base + TURN_RATE * n + spin
        cos_n, sin_n = jnp.cos(theta), jnp.sin(theta)
        cos_all.append(cos_n)
        sin_all.append(sin_n)

    def fill_kernels(n):
        rc, rs = radius * cos_all[n], radius * sin_all[n]
        for e in range(ENTRIES):
            y_rel = (rows_y + shift_y[e]).astype(f32)
            for b in range(BLADES):
                i = BLADES * e + b
                kern_y[n, e, :, b * nz : (b + 1) * nz] = taper_kernel(y_rel - rs[i : i + 1]) * valid[e]
                kern_z[n, e, :, b * nz : (b + 1) * nz] = taper_kernel(rows_z - rc[i : i + 1])

    cos_t, sin_t = jnp.cos(twist_ref[...]), jnp.sin(twist_ref[...])
    chord = FORCE_SCALE * chord_ref[...]
    zero_rows = jnp.zeros((ROWS - 2 * BLADES, nz), f32)

    lag_pack[0:BLADES] = lag_ref[...]
    lag_pack[BLADES : 2 * BLADES] = rate_ref[...]
    lag_pack[2 * BLADES : ROWS] = zero_rows
    lag_in[tile] = lag_pack[...]

    started = []

    def send(src, dst, send_sem, recv_sem, axis, other):
        copy = pltpu.make_async_remote_copy(
            src_ref=src,
            dst_ref=dst,
            send_sem=send_sem,
            recv_sem=recv_sem,
            device_id={axis: other},
            device_id_type=MESH,
        )
        copy.start()
        started.append(copy)
        return copy

    def send_lag(d, carry):
        pltpu.make_async_remote_copy(
            src_ref=lag_pack,
            dst_ref=lag_in.at[tile],
            send_sem=lag_send,
            recv_sem=lag_recv,
            device_id=peer(d),
            device_id_type=MESH,
        ).start()
        return carry

    def drain(ref, count, sem):
        block = ref.at[pl.ds(0, count)]
        pltpu.make_async_copy(block, block, sem).wait()

    def sample(n, src):
        cos_n, sin_n = cos_all[n], sin_all[n]
        sampled = [[], [], []]
        for e in range(ENTRIES):
            field = None
            for i in range(-2, 3):
                term = KERN_X[abs(i)] * src[:, load_x[e] + i]
                field = term if field is None else field + term
            inner = jnp.dot(
                field.reshape(3 * cy, nz),
                kern_z[n, e],
                precision=PRECISE,
                preferred_element_type=f32,
            )
            for c in range(3):
                reduced = jnp.sum(inner[c * cy : (c + 1) * cy] * kern_y[n, e], axis=0, keepdims=True)
                sampled[c] += [reduced[:, b * nz : (b + 1) * nz] for b in range(BLADES)]
        s = [jnp.concatenate(sampled[c] + [zero_rows], axis=0) for c in range(3)]
        part_out[n, 0] = s[0]
        part_out[n, 1] = s[1] * cos_n - s[2] * sin_n

    def faces(n, src):
        flat = src.reshape(3 * cx * cy, nz)
        for c in range(3):
            face_y[n, 0, c] = flat[pl.ds(c * cx * cy + cy - 1, cx, stride=cy), :]
            face_y[n, 1, c] = flat[pl.ds(c * cx * cy, cx, stride=cy), :]

    def send_parts(n):
        copies = [
            send(part_out.at[n], part_in.at[n, gy], ps_send.at[n, d], ps_recv.at[n, d], "gy", lax.rem(gy + d, ny))
            for d in range(1, ny)
        ]
        part_in[n, gy] = part_out[n]
        return copies

    def send_faces(n):
        return [
            send(face_y.at[n, 0], halo_y.at[n, 0], hy_send.at[n, 0], hy_recv.at[n, 0], "gy", up),
            send(face_y.at[n, 1], halo_y.at[n, 1], hy_send.at[n, 1], hy_recv.at[n, 1], "gy", down),
        ]

    def x_copies(n, src):
        east = pltpu.make_async_remote_copy(
            src_ref=src.at[:, cx - 1],
            dst_ref=halo_x.at[n, 0],
            send_sem=hx_send.at[n, 0],
            recv_sem=hx_recv.at[n, 0],
            device_id={"gx": lax.rem(gx + 1, nx)},
            device_id_type=MESH,
        )
        west = pltpu.make_async_remote_copy(
            src_ref=src.at[:, 0],
            dst_ref=halo_x.at[n, 1],
            send_sem=hx_send.at[n, 1],
            recv_sem=hx_recv.at[n, 1],
            device_id={"gx": lax.rem(gx + nx - 1, nx)},
            device_id_type=MESH,
        )
        return east, west

    def send_x(n, src):
        east, west = x_copies(n, src)

        @pl.when(gx < nx - 1)
        def _():
            east.start()

        @pl.when(gx > 0)
        def _():
            west.start()

    def wait_x(n, src):
        east, west = x_copies(n, src)

        @pl.when(gx > 0)
        def _():
            east.wait_recv()

        @pl.when(gx == 0)
        def _():
            halo_x[n, 0] = inflow_ref[...]

        @pl.when(gx < nx - 1)
        def _():
            west.wait_recv()

        @pl.when(gx == nx - 1)
        def _():
            halo_x[n, 1] = src[:, cx - 1]

    def wait_x_sent(n, src):
        east, west = x_copies(n, src)

        @pl.when(gx < nx - 1)
        def _():
            east.wait_send()

        @pl.when(gx > 0)
        def _():
            west.wait_send()

    lane = lax.broadcasted_iota(jnp.int32, (cy, nz), 1)
    row_c = lax.broadcasted_iota(jnp.int32, (cy, nz), 0)
    is_first_z, is_last_z = lane == 0, lane == nz - 1
    is_first_y, is_last_y = row_c == 0, row_c == cy - 1

    def moved(cur, prev, following, below, above):
        y_prev = jnp.where(is_first_y, below, pltpu.roll(cur, 1, 0))
        y_next = jnp.where(is_last_y, above, pltpu.roll(cur, cy - 1, 0))
        z_prev = jnp.where(is_first_z, 0.0, pltpu.roll(cur, 1, 1))
        z_next = jnp.where(is_last_z, cur, pltpu.roll(cur, nz - 1, 1))
        others = (following + (y_prev + y_next)) + (z_prev + z_next)
        return (
            (1.0 - ADVECT - 6.0 * DIFFUSE) * cur + (ADVECT + DIFFUSE) * prev + DIFFUSE * others
        )

    def interior(src, dst):
        def plane(x, carry):
            for c in range(3):
                dst[c, x] = moved(src[c, x], src[c, x - 1], src[c, x + 1], 0.0, 0.0)
            return carry

        lax.fori_loop(1, cx - 1, plane, 0, unroll=UNROLL)

    def totals(n):
        whole = []
        for c in range(2):
            total = part_out[n, c]
            for side, other_y in enumerate((down, up)):
                other = part_in[n, other_y, c]
                same, cross = mask_rows[side]
                swapped = jnp.where(first, pltpu.roll(other, ROWS - BLADES, 0), pltpu.roll(other, BLADES, 0))
                total = total + (same * other + cross * swapped)
            whole.append(total)
        return whole

    def relax(lag, rate, axial, turned):
        tangential = SPIN * radius - turned
        magnitude = jnp.sqrt(axial * axial + tangential * tangential + 1.0)
        lift_static = LIFT_SLOPE * (axial * cos_t - tangential * sin_t) / magnitude
        return lag + rate * (lift_static - lag), tangential, magnitude

    def fill_spread(n, lag, axial, tangential, magnitude):
        cos_b, sin_b = cos_all[n], sin_all[n]
        lift = chord * lag * magnitude
        forces = (-lift * tangential, lift * axial * cos_b, -lift * axial * sin_b)
        for e in range(ENTRIES):
            weighted = []
            for c in range(3):
                weighted.append(
                    jnp.concatenate(
                        [
                            forces[c][BLADES * e + b : BLADES * e + b + 1]
                            * kern_y[n, e, :, b * nz : (b + 1) * nz]
                            for b in range(BLADES)
                        ],
                        axis=1,
                    )
                )
            pushed = lax.dot_general(
                jnp.concatenate(weighted, axis=0),
                kern_z[n, e],
                (((1,), (1,)), ((), ())),
                precision=PRECISE,
                preferred_element_type=f32,
            )
            spread[n, e] = pushed.reshape(3, cy, nz)

    def finish(n, src, dst):
        def body_force(c, x):
            w0, w1 = weight_x(x - hub_x[0]), weight_x(x - hub_x[1])
            return w0 * spread[n, 0, c] + w1 * spread[n, 1, c]

        def halo_rows(c, x):
            return halo_y[n, 0, c, pl.ds(x, 1), :], halo_y[n, 1, c, pl.ds(x, 1), :]

        for c in range(3):
            below, above = halo_rows(c, 0)
            dst[c, 0] = moved(src[c, 0], halo_x[n, 0, c], src[c, 1], below, above) + body_force(c, 0)
            x = cx - 1
            below, above = halo_rows(c, x)
            dst[c, x] = moved(src[c, x], src[c, x - 1], halo_x[n, 1, c], below, above) + body_force(c, x)

        def plane_rest(x, carry):
            for c in range(3):
                below, above = halo_rows(c, x)
                edge = jnp.where(is_first_y, below, jnp.where(is_last_y, above, 0.0))
                dst[c, x] = dst[c, x] + (body_force(c, x) + DIFFUSE * edge)
            return carry

        lax.fori_loop(1, cx - 1, plane_rest, 0, unroll=UNROLL)

    def home_blocks(n):
        blocks = []
        for k in range(ny):
            axial, turned = part_in[n, k, 0], part_in[n, k, 1]
            blocks.append(jnp.where(first, axial, pltpu.roll(turned, BLADES, 0)))
            blocks.append(jnp.where(first, pltpu.roll(axial, ROWS - BLADES, 0), turned))
        return blocks

    def fill_home(n):
        blocks = home_blocks(n)
        for h in range(nx):
            wanted = BLADES * (h * ny + gy)
            total = None
            for k in range(ny):
                for f in range(ENTRIES):
                    hit = jnp.where(listed[k][f] == wanted, 1.0, 0.0).astype(f32)
                    term = hit * blocks[ENTRIES * k + f]
                    total = term if total is None else total + term
            home_out[h, n] = total

    fill_kernels(0)
    for copy in slabs:
        copy.wait()
    sample(0, grid0)
    faces(0, grid0)

    pl.semaphore_wait(barrier, devices - 1)
    lax.fori_loop(1, devices, send_lag, 0)
    parts = send_parts(0)
    halos = send_faces(0)
    send_x(0, grid0)
    fill_kernels(1)
    interior(grid0, grid1)
    for copy in parts:
        copy.wait_recv()
    axial, turned = totals(0)
    drain(lag_in, devices - 1, lag_recv)
    state_rows, rate_rows = [], []
    for e in range(ENTRIES):
        block = lag_in[jnp.maximum(rotor[e], 0)]
        state_rows.append(block[0:BLADES])
        rate_rows.append(block[BLADES : 2 * BLADES])
    lag = jnp.concatenate(state_rows + [zero_rows], axis=0)
    rate = jnp.concatenate(rate_rows + [zero_rows], axis=0)
    lag, tangential, magnitude = relax(lag, rate, axial, turned)
    fill_spread(0, lag, axial, tangential, magnitude)
    for copy in halos:
        copy.wait_recv()
    wait_x(0, grid0)
    finish(0, grid0, grid1)

    sample(1, grid1)
    parts = send_parts(1)
    faces(1, grid1)
    halos = send_faces(1)
    send_x(1, grid1)
    fill_home(0)
    interior(grid1, out_ref)
    for copy in parts:
        copy.wait_recv()
    fill_home(1)
    homes = [
        send(
            home_out.at[lax.rem(gx + d, nx)],
            home_in.at[gx],
            home_send.at[d],
            home_recv.at[d],
            "gx",
            lax.rem(gx + d, nx),
        )
        for d in range(1, nx)
    ]
    home_in[gx] = home_out[gx]
    axial, turned = totals(1)
    lag, tangential, magnitude = relax(lag, rate, axial, turned)
    fill_spread(1, lag, axial, tangential, magnitude)
    for copy in halos:
        copy.wait_recv()
    wait_x(1, grid1)
    finish(1, grid1, out_ref)

    for copy in homes:
        copy.wait_recv()
    own = lag_pack[...]
    state, own_rate = own, pltpu.roll(own, ROWS - BLADES, 0)
    for n in range(STEPS):
        total = home_in[0, n]
        for h in range(1, nx):
            total = total + home_in[h, n]
        state, _, _ = relax(state, own_rate, total, pltpu.roll(total, ROWS - BLADES, 0))
    state_ref[...] = state[0:BLADES]
    drain(lag_in, devices - 1, lag_send)
    for n, src in ((0, grid0), (1, grid1)):
        wait_x_sent(n, src)
    for copy in started:
        copy.wait_send()


def store_kernel(vel_ref, state_ref, vel_hbm, state_hbm, sem):
    width = vel_ref.shape[1] // CHUNKS
    copies = [
        pltpu.make_async_copy(
            vel_ref.at[:, pl.ds(i * width, width)], vel_hbm.at[:, pl.ds(i * width, width)], sem.at[i]
        )
        for i in range(CHUNKS)
    ]
    copies.append(pltpu.make_async_copy(state_ref, state_hbm, sem.at[CHUNKS]))
    for copy in copies:
        copy.start()
    for copy in copies:
        copy.wait()


def per_device(
    velocity, inflow, azimuth, positions, crossings, lag_state, lag_rate, chord_len, twist_angle
):
    nx = lax.axis_size("gx")
    ny = lax.axis_size("gy")
    comps, cx, cy, nz = velocity.shape
    own, sections = lag_state.shape
    assert comps == 3 and own == BLADES and sections == nz
    f32 = jnp.float32
    grid = pltpu.VMEM((3, cx, cy, nz), f32)
    dma = pltpu.SemaphoreType.DMA
    hbm = pl.BlockSpec(memory_space=pltpu.HBM)
    vmem = pl.BlockSpec(memory_space=pltpu.VMEM)
    moved, state = pl.pallas_call(
        functools.partial(farm_kernel, nx, ny),
        out_shape=(pltpu.VMEM(velocity.shape, f32), pltpu.VMEM(lag_state.shape, f32)),
        in_specs=[hbm] * 9,
        out_specs=(vmem, vmem),
        scratch_shapes=[
            pltpu.VMEM(inflow.shape, f32),
            pltpu.SMEM(azimuth.shape, f32),
            pltpu.SMEM(positions.shape[::-1], jnp.int32),
            pltpu.SMEM(crossings.shape[::-1], jnp.int32),
            pltpu.VMEM(lag_state.shape, f32),
            pltpu.VMEM(lag_state.shape, f32),
            pltpu.VMEM((1, sections), f32),
            pltpu.VMEM((1, sections), f32),
            grid,
            grid,
            pltpu.VMEM((STEPS, 2, 3, cy, nz), f32),
            pltpu.VMEM((STEPS, 2, 3, cx, nz), f32),
            pltpu.VMEM((STEPS, 2, 3, cx, nz), f32),
            pltpu.VMEM((STEPS, 2, ROWS, nz), f32),
            pltpu.VMEM((STEPS, ny, 2, ROWS, nz), f32),
            pltpu.VMEM((STEPS, ENTRIES, cy, BLADES * nz), f32),
            pltpu.VMEM((STEPS, ENTRIES, nz, BLADES * nz), f32),
            pltpu.VMEM((STEPS, ENTRIES, 3, cy, nz), f32),
            pltpu.VMEM((ROWS, nz), f32),
            pltpu.VMEM((nx * ny, ROWS, nz), f32),
            pltpu.VMEM((nx, STEPS, ROWS, nz), f32),
            pltpu.VMEM((nx, STEPS, ROWS, nz), f32),
            dma((8,)),
            dma((3,)),
            dma((STEPS, 2)),
            dma((STEPS, 2)),
            dma((STEPS, 2)),
            dma((STEPS, 2)),
            dma((STEPS, ny)),
            dma((STEPS, ny)),
            dma,
            dma,
            dma((nx,)),
            dma((nx,)),
        ],
        compiler_params=pltpu.CompilerParams(
            collective_id=0, has_side_effects=True, vmem_limit_bytes=30 * 1024 * 1024
        ),
        cost_estimate=pl.CostEstimate(
            flops=50_000_000, bytes_accessed=8 * velocity.size, transcendentals=500_000
        ),
    )(
        *(
            pltpu.with_memory_space_constraint(source, pltpu.HBM)
            for source in (
                velocity,
                inflow,
                azimuth,
                positions.T,
                crossings.T,
                lag_state,
                lag_rate,
                chord_len.reshape(1, sections),
                twist_angle.reshape(1, sections),
            )
        )
    )
    anywhere = pl.BlockSpec(memory_space=pl.ANY)
    return pl.pallas_call(
        store_kernel,
        out_shape=(
            jax.ShapeDtypeStruct(velocity.shape, f32),
            jax.ShapeDtypeStruct(lag_state.shape, f32),
        ),
        in_specs=[anywhere] * 2,
        out_specs=(pl.BlockSpec(memory_space=pltpu.HBM),) * 2,
        scratch_shapes=[dma((CHUNKS + 1,))],
        compiler_params=pltpu.CompilerParams(vmem_limit_bytes=16 * 1024 * 1024),
    )(
        pltpu.with_memory_space_constraint(moved, pltpu.VMEM),
        pltpu.with_memory_space_constraint(state, pltpu.VMEM),
    )


def solution(mesh):
    return jax.shard_map(
        per_device,
        mesh=mesh,
        in_specs=(
            P(None, "gx", "gy", None),
            P(None, "gy", None),
            P(),
            P(),
            P(),
            P(("gx", "gy"), None),
            P(("gx", "gy"), None),
            P(),
            P(),
        ),
        out_specs=(P(None, "gx", "gy", None), P(("gx", "gy"), None)),
        check_vma=False,
    )
```

```python
import functools
import math

import jax
import jax.numpy as jnp
from jax import lax
from jax.experimental import pallas as pl
from jax.experimental.pallas import tpu as pltpu
from jax.sharding import PartitionSpec as P

RADIUS = 12
HUB = 15
STEPS = 2
EPSILON = 2.0
SUPPORT = 3.0
TURN_RATE = 0.1
SPIN = 0.25
LIFT_SLOPE = 2.0 * math.pi
FORCE_SCALE = 0.15
ADVECT = 0.5
DIFFUSE = 0.05
PRECISE = lax.Precision.HIGH
MESH = pl.DeviceIdType.MESH
BLADES = 3
ENTRIES = 2
ROWS = 8
UNROLL = 4
SLAB = 8
CHUNKS = 4


def taper_const(distance):
    square = distance * distance
    term = max(1.0 - square / (SUPPORT * SUPPORT), 0.0)
    return math.exp(-square / EPSILON**2) * term * term / (EPSILON * math.sqrt(math.pi))


KERN_X = [taper_const(float(i)) for i in range(3)]


def taper_kernel(distance):
    square = distance * distance
    term = jnp.maximum(1.0 - square * (1.0 / (SUPPORT * SUPPORT)), 0.0)
    return (
        jnp.exp(square * (-1.0 / (EPSILON * EPSILON)))
        * (term * term)
        * (1.0 / (EPSILON * math.sqrt(math.pi)))
    )


def weight_x(offset):
    dist = jnp.abs(offset)
    return jnp.where(
        dist == 0,
        KERN_X[0],
        jnp.where(dist == 1, KERN_X[1], jnp.where(dist == 2, KERN_X[2], 0.0)),
    ).astype(jnp.float32)


def farm_kernel(
    nx,
    ny,
    vel_hbm,
    inflow_hbm,
    az_hbm,
    pos_hbm,
    cross_hbm,
    lag_hbm,
    rate_hbm,
    chord_hbm,
    twist_hbm,
    out_ref,
    state_ref,
    inflow_ref,
    az_ref,
    pos_ref,
    cross_ref,
    lag_ref,
    rate_ref,
    chord_ref,
    twist_ref,
    grid0,
    grid1,
    halo_x,
    halo_y,
    face_y,
    part_out,
    part_in,
    kern_y,
    kern_z,
    spread,
    lag_pack,
    lag_col,
    lag_in,
    rows_out,
    rows_in,
    home_out,
    home_in,
    small_sem,
    load_sem,
    hx_send,
    hx_recv,
    hy_send,
    hy_recv,
    ps_send,
    ps_recv,
    ly_send,
    ly_recv,
    lx_send,
    lx_recv,
    rw_send,
    rw_recv,
    home_send,
    home_recv,
):
    f32 = jnp.float32
    _, cx, cy, nz = grid0.shape
    total_y = cy * ny
    gx = lax.axis_index("gx")
    gy = lax.axis_index("gy")
    tile = gx * ny + gy
    up = lax.rem(gy + 1, ny)
    down = lax.rem(gy + ny - 1, ny)

    smalls = [
        pltpu.make_async_copy(source, target, small_sem.at[i])
        for i, (source, target) in enumerate(
            (
                (az_hbm, az_ref),
                (pos_hbm, pos_ref),
                (cross_hbm, cross_ref),
                (lag_hbm, lag_ref),
                (rate_hbm, rate_ref),
                (chord_hbm, chord_ref),
                (twist_hbm, twist_ref),
                (inflow_hbm, inflow_ref),
            )
        )
    ]
    for copy in smalls:
        copy.start()
    slabs = [
        pltpu.make_async_copy(vel_hbm.at[:, :, rows], grid0.at[:, :, rows], load_sem.at[i])
        for i, rows in enumerate((pl.ds(cy - SLAB, SLAB), pl.ds(0, SLAB), pl.ds(SLAB, cy - 2 * SLAB)))
    ]
    for copy in slabs:
        copy.start()

    barrier = pltpu.get_barrier_semaphore()

    for d in range(1, ny):
        pl.semaphore_signal(
            barrier, inc=1, device_id={"gy": lax.rem(gy + d, ny)}, device_id_type=MESH
        )
    for d in range(1, nx):
        pl.semaphore_signal(
            barrier, inc=1, device_id={"gx": lax.rem(gx + d, nx)}, device_id_type=MESH
        )

    for copy in smalls:
        copy.wait()

    rotor, hub_x, load_x, shift_y, valid, az = [], [], [], [], [], []
    for e in range(ENTRIES):
        blade = cross_ref[BLADES * e, tile]
        r = jnp.where(blade >= 0, blade, 0) // BLADES
        rotor.append(jnp.where(blade >= 0, r, -1))
        valid.append(jnp.where(blade >= 0, 1.0, 0.0).astype(f32))
        hub_x.append(jnp.where(blade >= 0, pos_ref[0, r] - gx * cx, 2))
        load_x.append(jnp.clip(hub_x[e], 2, cx - 3))
        off = gy * cy - pos_ref[1, r] + total_y + total_y // 2
        shift_y.append(lax.rem(off, total_y) - total_y // 2)
        az.append(az_ref[r])

    listed = [[cross_ref[BLADES * f, gx * ny + k] for f in range(ENTRIES)] for k in range(ny)]

    def matches(other):
        found = []
        for f in range(ENTRIES):
            blade = cross_ref[BLADES * f, other]
            found.append(jnp.where(blade >= 0, jnp.where(blade >= 0, blade, 0) // BLADES, -2))
        return [
            [jnp.where(rotor[e] == found[f], 1.0, 0.0).astype(f32) for f in range(ENTRIES)]
            for e in range(ENTRIES)
        ]

    row = lax.broadcasted_iota(jnp.int32, (ROWS, nz), 0)
    first = row < BLADES
    lane8 = lax.broadcasted_iota(jnp.int32, (ROWS, nz), 1).astype(f32)
    radius = RADIUS * (lane8 + 0.5) / nz
    spin = jnp.where(first, row, row - BLADES).astype(f32) * (2.0 * math.pi / 3.0)
    base = jnp.where(first, az[0], az[1])
    mask_rows = []
    for other in (gx * ny + down, gx * ny + up):
        m = matches(other)
        mask_rows.append(
            (jnp.where(first, m[0][0], m[1][1]), jnp.where(first, m[0][1], m[1][0]))
        )
    cos_all, sin_all = [], []
    rows_y = lax.broadcasted_iota(jnp.int32, (cy, nz), 0)
    rows_z = lax.broadcasted_iota(jnp.int32, (nz, nz), 0).astype(f32) - HUB
    for n in range(STEPS):
        theta = base + TURN_RATE * n + spin
        cos_n, sin_n = jnp.cos(theta), jnp.sin(theta)
        cos_all.append(cos_n)
        sin_all.append(sin_n)

    def fill_kernels(n):
        rc, rs = radius * cos_all[n], radius * sin_all[n]
        for e in range(ENTRIES):
            y_rel = (rows_y + shift_y[e]).astype(f32)
            for b in range(BLADES):
                i = BLADES * e + b
                kern_y[n, e, :, b * nz : (b + 1) * nz] = taper_kernel(y_rel - rs[i : i + 1]) * valid[e]
                kern_z[n, e, :, b * nz : (b + 1) * nz] = taper_kernel(rows_z - rc[i : i + 1])

    cos_t, sin_t = jnp.cos(twist_ref[...]), jnp.sin(twist_ref[...])
    chord = FORCE_SCALE * chord_ref[...]
    zero_rows = jnp.zeros((ROWS - 2 * BLADES, nz), f32)

    lag_pack[0:BLADES] = lag_ref[...]
    lag_pack[BLADES : 2 * BLADES] = rate_ref[...]
    lag_pack[2 * BLADES : ROWS] = zero_rows

    started = []

    def send(src, dst, send_sem, recv_sem, axis, other):
        copy = pltpu.make_async_remote_copy(
            src_ref=src,
            dst_ref=dst,
            send_sem=send_sem,
            recv_sem=recv_sem,
            device_id={axis: other},
            device_id_type=MESH,
        )
        copy.start()
        started.append(copy)
        return copy

    def send_lag_column():
        copies = [
            send(lag_pack, lag_col.at[gy], ly_send.at[d], ly_recv.at[d], "gy", lax.rem(gy + d, ny))
            for d in range(1, ny)
        ]
        lag_col[gy] = lag_pack[...]
        return copies

    def send_lag_block():
        copies = [
            send(lag_col, lag_in.at[gx], lx_send.at[d], lx_recv.at[d], "gx", lax.rem(gx + d, nx))
            for d in range(1, nx)
        ]
        lag_in[gx] = lag_col[...]
        return copies

    def sample(n, src):
        cos_n, sin_n = cos_all[n], sin_all[n]
        sampled = [[], [], []]
        for e in range(ENTRIES):
            field = None
            for i in range(-2, 3):
                term = KERN_X[abs(i)] * src[:, load_x[e] + i]
                field = term if field is None else field + term
            inner = jnp.dot(
                field.reshape(3 * cy, nz),
                kern_z[n, e],
                precision=PRECISE,
                preferred_element_type=f32,
            )
            for c in range(3):
                reduced = jnp.sum(inner[c * cy : (c + 1) * cy] * kern_y[n, e], axis=0, keepdims=True)
                sampled[c] += [reduced[:, b * nz : (b + 1) * nz] for b in range(BLADES)]
        s = [jnp.concatenate(sampled[c] + [zero_rows], axis=0) for c in range(3)]
        part_out[n, 0] = s[0]
        part_out[n, 1] = s[1] * cos_n - s[2] * sin_n

    def faces(n, src):
        flat = src.reshape(3 * cx * cy, nz)
        for c in range(3):
            face_y[n, 0, c] = flat[pl.ds(c * cx * cy + cy - 1, cx, stride=cy), :]
            face_y[n, 1, c] = flat[pl.ds(c * cx * cy, cx, stride=cy), :]

    def send_parts(n):
        copies = [
            send(part_out.at[n], part_in.at[n, gy], ps_send.at[n, d], ps_recv.at[n, d], "gy", lax.rem(gy + d, ny))
            for d in range(1, ny)
        ]
        part_in[n, gy] = part_out[n]
        return copies

    def send_faces(n):
        return [
            send(face_y.at[n, 0], halo_y.at[n, 0], hy_send.at[n, 0], hy_recv.at[n, 0], "gy", up),
            send(face_y.at[n, 1], halo_y.at[n, 1], hy_send.at[n, 1], hy_recv.at[n, 1], "gy", down),
        ]

    def x_copies(n, src):
        east = pltpu.make_async_remote_copy(
            src_ref=src.at[:, cx - 1],
            dst_ref=halo_x.at[n, 0],
            send_sem=hx_send.at[n, 0],
            recv_sem=hx_recv.at[n, 0],
            device_id={"gx": lax.rem(gx + 1, nx)},
            device_id_type=MESH,
        )
        west = pltpu.make_async_remote_copy(
            src_ref=src.at[:, 0],
            dst_ref=halo_x.at[n, 1],
            send_sem=hx_send.at[n, 1],
            recv_sem=hx_recv.at[n, 1],
            device_id={"gx": lax.rem(gx + nx - 1, nx)},
            device_id_type=MESH,
        )
        return east, west

    def send_x(n, src):
        east, west = x_copies(n, src)

        @pl.when(gx < nx - 1)
        def _():
            east.start()

        @pl.when(gx > 0)
        def _():
            west.start()

    def wait_x(n, src):
        east, west = x_copies(n, src)

        @pl.when(gx > 0)
        def _():
            east.wait_recv()

        @pl.when(gx == 0)
        def _():
            halo_x[n, 0] = inflow_ref[...]

        @pl.when(gx < nx - 1)
        def _():
            west.wait_recv()

        @pl.when(gx == nx - 1)
        def _():
            halo_x[n, 1] = src[:, cx - 1]

    def wait_x_sent(n, src):
        east, west = x_copies(n, src)

        @pl.when(gx < nx - 1)
        def _():
            east.wait_send()

        @pl.when(gx > 0)
        def _():
            west.wait_send()

    lane = lax.broadcasted_iota(jnp.int32, (cy, nz), 1)
    row_c = lax.broadcasted_iota(jnp.int32, (cy, nz), 0)
    is_first_z, is_last_z = lane == 0, lane == nz - 1
    is_first_y, is_last_y = row_c == 0, row_c == cy - 1

    def moved(cur, prev, following, below, above):
        y_prev = jnp.where(is_first_y, below, pltpu.roll(cur, 1, 0))
        y_next = jnp.where(is_last_y, above, pltpu.roll(cur, cy - 1, 0))
        z_prev = jnp.where(is_first_z, 0.0, pltpu.roll(cur, 1, 1))
        z_next = jnp.where(is_last_z, cur, pltpu.roll(cur, nz - 1, 1))
        others = (following + (y_prev + y_next)) + (z_prev + z_next)
        return (
            (1.0 - ADVECT - 6.0 * DIFFUSE) * cur + (ADVECT + DIFFUSE) * prev + DIFFUSE * others
        )

    def interior(src, dst):
        def plane(x, carry):
            for c in range(3):
                dst[c, x] = moved(src[c, x], src[c, x - 1], src[c, x + 1], 0.0, 0.0)
            return carry

        for c in range(3):
            dst[c, 0] = moved(src[c, 0], 0.0, src[c, 1], 0.0, 0.0)
        lax.fori_loop(1, cx - 1, plane, 0, unroll=UNROLL)
        for c in range(3):
            dst[c, cx - 1] = moved(src[c, cx - 1], src[c, cx - 2], 0.0, 0.0, 0.0)

    def totals(n):
        whole = []
        for c in range(2):
            total = part_out[n, c]
            for side, other_y in enumerate((down, up)):
                other = part_in[n, other_y, c]
                same, cross = mask_rows[side]
                swapped = jnp.where(first, pltpu.roll(other, ROWS - BLADES, 0), pltpu.roll(other, BLADES, 0))
                total = total + (same * other + cross * swapped)
            whole.append(total)
        return whole

    def relax(lag, rate, axial, turned):
        tangential = SPIN * radius - turned
        magnitude = jnp.sqrt(axial * axial + tangential * tangential + 1.0)
        lift_static = LIFT_SLOPE * (axial * cos_t - tangential * sin_t) / magnitude
        return lag + rate * (lift_static - lag), tangential, magnitude

    def fill_spread(n, lag, axial, tangential, magnitude):
        cos_b, sin_b = cos_all[n], sin_all[n]
        lift = chord * lag * magnitude
        forces = (-lift * tangential, lift * axial * cos_b, -lift * axial * sin_b)
        for e in range(ENTRIES):
            weighted = []
            for c in range(3):
                weighted.append(
                    jnp.concatenate(
                        [
                            forces[c][BLADES * e + b : BLADES * e + b + 1]
                            * kern_y[n, e, :, b * nz : (b + 1) * nz]
                            for b in range(BLADES)
                        ],
                        axis=1,
                    )
                )
            pushed = lax.dot_general(
                jnp.concatenate(weighted, axis=0),
                kern_z[n, e],
                (((1,), (1,)), ((), ())),
                precision=PRECISE,
                preferred_element_type=f32,
            )
            spread[n, e] = pushed.reshape(3, cy, nz)

    def finish(n, dst):
        def body_force(c, x):
            w0, w1 = weight_x(x - hub_x[0]), weight_x(x - hub_x[1])
            return w0 * spread[n, 0, c] + w1 * spread[n, 1, c]

        def halo_rows(c, x):
            return halo_y[n, 0, c, pl.ds(x, 1), :], halo_y[n, 1, c, pl.ds(x, 1), :]

        def plane_rest(x, carry):
            for c in range(3):
                below, above = halo_rows(c, x)
                edge = jnp.where(is_first_y, below, jnp.where(is_last_y, above, 0.0))
                dst[c, x] = dst[c, x] + (body_force(c, x) + DIFFUSE * edge)
            return carry

        lax.fori_loop(0, cx, plane_rest, 0, unroll=UNROLL)
        for c in range(3):
            dst[c, 0] = dst[c, 0] + (ADVECT + DIFFUSE) * halo_x[n, 0, c]
            dst[c, cx - 1] = dst[c, cx - 1] + DIFFUSE * halo_x[n, 1, c]

    def send_rows():
        for side, edge in enumerate((cy - 1, 0)):
            for c in range(3):
                for e in range(ENTRIES):
                    rows_out[side, c, e : e + 1] = spread[0, e, c, edge : edge + 1]
                for k in range(2):
                    rows_out[side, c, 2 + k : 3 + k] = halo_x[0, k, c, edge : edge + 1]
        return [
            send(rows_out.at[0], rows_in.at[0], rw_send.at[0], rw_recv.at[0], "gy", up),
            send(rows_out.at[1], rows_in.at[1], rw_send.at[1], rw_recv.at[1], "gy", down),
        ]

    def complete_halo():
        plane_id = lax.broadcasted_iota(jnp.int32, (cx, nz), 0)
        at_low = jnp.where(plane_id == 0, ADVECT + DIFFUSE, 0.0).astype(f32)
        at_high = jnp.where(plane_id == cx - 1, DIFFUSE, 0.0).astype(f32)
        for side, other in enumerate((down, up)):
            weights = []
            for f in range(ENTRIES):
                blade = cross_ref[BLADES * f, gx * ny + other]
                r = jnp.where(blade >= 0, blade, 0) // BLADES
                weights.append(weight_x(plane_id - (pos_ref[0, r] - gx * cx)))
            weights += [at_low, at_high]
            for c in range(3):
                total = halo_y[1, side, c] + DIFFUSE * face_y[0, 1 - side, c]
                for k in range(4):
                    total = total + weights[k] * rows_in[side, c, k : k + 1]
                halo_y[1, side, c] = total

    def home_blocks(n):
        blocks = []
        for k in range(ny):
            axial, turned = part_in[n, k, 0], part_in[n, k, 1]
            blocks.append(jnp.where(first, axial, pltpu.roll(turned, BLADES, 0)))
            blocks.append(jnp.where(first, pltpu.roll(axial, ROWS - BLADES, 0), turned))
        return blocks

    def fill_home(n):
        blocks = home_blocks(n)
        for h in range(nx):
            wanted = BLADES * (h * ny + gy)
            total = None
            for k in range(ny):
                for f in range(ENTRIES):
                    hit = jnp.where(listed[k][f] == wanted, 1.0, 0.0).astype(f32)
                    term = hit * blocks[ENTRIES * k + f]
                    total = term if total is None else total + term
            home_out[h, n] = total

    fill_kernels(0)
    for copy in slabs:
        copy.wait()
    sample(0, grid0)
    faces(0, grid0)

    pl.semaphore_wait(barrier, nx - 1 + ny - 1)
    lags = send_lag_column()
    parts = send_parts(0)
    halos = send_faces(0)
    send_x(0, grid0)
    interior(grid0, grid1)
    faces(1, grid1)
    late_halos = send_faces(1)
    fill_kernels(1)
    for copy in lags:
        copy.wait_recv()
    lags = send_lag_block()
    for copy in parts:
        copy.wait_recv()
    axial, turned = totals(0)
    for copy in lags:
        copy.wait_recv()
    state_rows, rate_rows = [], []
    for e in range(ENTRIES):
        r = jnp.maximum(rotor[e], 0)
        block = lag_in[r // ny, lax.rem(r, ny)]
        state_rows.append(block[0:BLADES])
        rate_rows.append(block[BLADES : 2 * BLADES])
    lag = jnp.concatenate(state_rows + [zero_rows], axis=0)
    rate = jnp.concatenate(rate_rows + [zero_rows], axis=0)
    lag, tangential, magnitude = relax(lag, rate, axial, turned)
    fill_spread(0, lag, axial, tangential, magnitude)
    wait_x(0, grid0)
    rows = send_rows()
    for copy in halos:
        copy.wait_recv()
    finish(0, grid1)

    sample(1, grid1)
    parts = send_parts(1)
    send_x(1, grid1)
    fill_home(0)
    interior(grid1, out_ref)
    for copy in parts:
        copy.wait_recv()
    fill_home(1)
    homes = [
        send(
            home_out.at[lax.rem(gx + d, nx)],
            home_in.at[gx],
            home_send.at[d],
            home_recv.at[d],
            "gx",
            lax.rem(gx + d, nx),
        )
        for d in range(1, nx)
    ]
    home_in[gx] = home_out[gx]
    axial, turned = totals(1)
    lag, tangential, magnitude = relax(lag, rate, axial, turned)
    fill_spread(1, lag, axial, tangential, magnitude)
    wait_x(1, grid1)
    for copy in rows + late_halos:
        copy.wait_recv()
    complete_halo()
    finish(1, out_ref)

    for copy in homes:
        copy.wait_recv()
    own = lag_pack[...]
    state, own_rate = own, pltpu.roll(own, ROWS - BLADES, 0)
    for n in range(STEPS):
        total = home_in[0, n]
        for h in range(1, nx):
            total = total + home_in[h, n]
        state, _, _ = relax(state, own_rate, total, pltpu.roll(total, ROWS - BLADES, 0))
    state_ref[...] = state[0:BLADES]
    for n, src in ((0, grid0), (1, grid1)):
        wait_x_sent(n, src)
    for copy in started:
        copy.wait_send()


def store_kernel(vel_ref, state_ref, vel_hbm, state_hbm, sem):
    width = vel_ref.shape[1] // CHUNKS
    copies = [
        pltpu.make_async_copy(
            vel_ref.at[:, pl.ds(i * width, width)], vel_hbm.at[:, pl.ds(i * width, width)], sem.at[i]
        )
        for i in range(CHUNKS)
    ]
    copies.append(pltpu.make_async_copy(state_ref, state_hbm, sem.at[CHUNKS]))
    for copy in copies:
        copy.start()
    for copy in copies:
        copy.wait()


def per_device(
    velocity, inflow, azimuth, positions, crossings, lag_state, lag_rate, chord_len, twist_angle
):
    nx = lax.axis_size("gx")
    ny = lax.axis_size("gy")
    comps, cx, cy, nz = velocity.shape
    own, sections = lag_state.shape
    assert comps == 3 and own == BLADES and sections == nz
    f32 = jnp.float32
    grid = pltpu.VMEM((3, cx, cy, nz), f32)
    dma = pltpu.SemaphoreType.DMA
    hbm = pl.BlockSpec(memory_space=pltpu.HBM)
    vmem = pl.BlockSpec(memory_space=pltpu.VMEM)
    moved, state = pl.pallas_call(
        functools.partial(farm_kernel, nx, ny),
        out_shape=(pltpu.VMEM(velocity.shape, f32), pltpu.VMEM(lag_state.shape, f32)),
        in_specs=[hbm] * 9,
        out_specs=(vmem, vmem),
        scratch_shapes=[
            pltpu.VMEM(inflow.shape, f32),
            pltpu.SMEM(azimuth.shape, f32),
            pltpu.SMEM(positions.shape[::-1], jnp.int32),
            pltpu.SMEM(crossings.shape[::-1], jnp.int32),
            pltpu.VMEM(lag_state.shape, f32),
            pltpu.VMEM(lag_state.shape, f32),
            pltpu.VMEM((1, sections), f32),
            pltpu.VMEM((1, sections), f32),
            grid,
            grid,
            pltpu.VMEM((STEPS, 2, 3, cy, nz), f32),
            pltpu.VMEM((STEPS, 2, 3, cx, nz), f32),
            pltpu.VMEM((STEPS, 2, 3, cx, nz), f32),
            pltpu.VMEM((STEPS, 2, ROWS, nz), f32),
            pltpu.VMEM((STEPS, ny, 2, ROWS, nz), f32),
            pltpu.VMEM((STEPS, ENTRIES, cy, BLADES * nz), f32),
            pltpu.VMEM((STEPS, ENTRIES, nz, BLADES * nz), f32),
            pltpu.VMEM((STEPS, ENTRIES, 3, cy, nz), f32),
            pltpu.VMEM((ROWS, nz), f32),
            pltpu.VMEM((ny, ROWS, nz), f32),
            pltpu.VMEM((nx, ny, ROWS, nz), f32),
            pltpu.VMEM((2, 3, 4, nz), f32),
            pltpu.VMEM((2, 3, 4, nz), f32),
            pltpu.VMEM((nx, STEPS, ROWS, nz), f32),
            pltpu.VMEM((nx, STEPS, ROWS, nz), f32),
            dma((8,)),
            dma((3,)),
            dma((STEPS, 2)),
            dma((STEPS, 2)),
            dma((STEPS, 2)),
            dma((STEPS, 2)),
            dma((STEPS, ny)),
            dma((STEPS, ny)),
            dma((ny,)),
            dma((ny,)),
            dma((nx,)),
            dma((nx,)),
            dma((2,)),
            dma((2,)),
            dma((nx,)),
            dma((nx,)),
        ],
        compiler_params=pltpu.CompilerParams(
            collective_id=0, has_side_effects=True, vmem_limit_bytes=30 * 1024 * 1024
        ),
        cost_estimate=pl.CostEstimate(
            flops=50_000_000, bytes_accessed=8 * velocity.size, transcendentals=500_000
        ),
    )(
        *(
            pltpu.with_memory_space_constraint(source, pltpu.HBM)
            for source in (
                velocity,
                inflow,
                azimuth,
                positions.T,
                crossings.T,
                lag_state,
                lag_rate,
                chord_len.reshape(1, sections),
                twist_angle.reshape(1, sections),
            )
        )
    )
    anywhere = pl.BlockSpec(memory_space=pl.ANY)
    return pl.pallas_call(
        store_kernel,
        out_shape=(
            jax.ShapeDtypeStruct(velocity.shape, f32),
            jax.ShapeDtypeStruct(lag_state.shape, f32),
        ),
        in_specs=[anywhere] * 2,
        out_specs=(pl.BlockSpec(memory_space=pltpu.HBM),) * 2,
        scratch_shapes=[dma((CHUNKS + 1,))],
        compiler_params=pltpu.CompilerParams(vmem_limit_bytes=16 * 1024 * 1024),
    )(
        pltpu.with_memory_space_constraint(moved, pltpu.VMEM),
        pltpu.with_memory_space_constraint(state, pltpu.VMEM),
    )


def solution(mesh):
    return jax.shard_map(
        per_device,
        mesh=mesh,
        in_specs=(
            P(None, "gx", "gy", None),
            P(None, "gy", None),
            P(),
            P(),
            P(),
            P(("gx", "gy"), None),
            P(("gx", "gy"), None),
            P(),
            P(),
        ),
        out_specs=(P(None, "gx", "gy", None), P(("gx", "gy"), None)),
        check_vma=False,
    )
```

```python
import functools
import math

import jax
import jax.numpy as jnp
from jax import lax
from jax.experimental import pallas as pl
from jax.experimental.pallas import tpu as pltpu
from jax.sharding import PartitionSpec as P

RADIUS = 12
HUB = 15
STEPS = 2
EPSILON = 2.0
SUPPORT = 3.0
TURN_RATE = 0.1
SPIN = 0.25
LIFT_SLOPE = 2.0 * math.pi
FORCE_SCALE = 0.15
ADVECT = 0.5
DIFFUSE = 0.05
PRECISE = lax.Precision.HIGH
MESH = pl.DeviceIdType.MESH
CENTRE = round((1.0 - ADVECT - 6.0 * DIFFUSE) / DIFFUSE)
LEAD = (ADVECT + DIFFUSE) / DIFFUSE
GROUP = 16
BLADES = 3
ENTRIES = 2
ROWS = 8
UNROLL = 4
SLAB = 8
CHUNKS = 4


def taper_const(distance):
    square = distance * distance
    term = max(1.0 - square / (SUPPORT * SUPPORT), 0.0)
    return math.exp(-square / EPSILON**2) * term * term / (EPSILON * math.sqrt(math.pi))


KERN_X = [taper_const(float(i)) for i in range(3)]
PAIR_X = [
    sum(KERN_X[abs(i)] * KERN_X[abs(i + d)] for i in range(-2, 3) if abs(i + d) <= 2) for d in range(5)
]


def taper_kernel(distance):
    square = distance * distance
    term = jnp.maximum(1.0 - square * (1.0 / (SUPPORT * SUPPORT)), 0.0)
    return (
        jnp.exp(square * (-1.0 / (EPSILON * EPSILON)))
        * (term * term)
        * (1.0 / (EPSILON * math.sqrt(math.pi)))
    )


def weight_x(offset):
    dist = jnp.abs(offset)
    return jnp.where(
        dist == 0,
        KERN_X[0],
        jnp.where(dist == 1, KERN_X[1], jnp.where(dist == 2, KERN_X[2], 0.0)),
    ).astype(jnp.float32)


def pair_x(offset):
    dist = jnp.abs(offset)
    total = jnp.where(dist == 0, PAIR_X[0], 0.0)
    for d in range(1, 5):
        total = jnp.where(dist == d, PAIR_X[d], total)
    return total.astype(jnp.float32)


def farm_kernel(
    nx,
    ny,
    vel_hbm,
    inflow_hbm,
    az_hbm,
    pos_hbm,
    cross_hbm,
    lag_hbm,
    rate_hbm,
    chord_hbm,
    twist_hbm,
    out_ref,
    state_ref,
    inflow_ref,
    az_ref,
    pos_ref,
    cross_ref,
    lag_ref,
    rate_ref,
    chord_ref,
    twist_ref,
    grid0,
    grid1,
    halo_x,
    halo_y,
    late_y,
    face_y,
    part_out,
    part_in,
    kern_y,
    kern_z,
    spread,
    lag_pack,
    lag_col,
    lag_in,
    rows_out,
    rows_in,
    home_out,
    home_in,
    small_sem,
    load_sem,
    hx_send,
    hx_recv,
    hy_send,
    hy_recv,
    ps_send,
    ps_recv,
    ly_send,
    ly_recv,
    lx_send,
    lx_recv,
    rw_send,
    rw_recv,
    home_send,
    home_recv,
):
    f32 = jnp.float32
    _, cx, cy, nz = grid0.shape
    total_y = cy * ny
    gx = lax.axis_index("gx")
    gy = lax.axis_index("gy")
    tile = gx * ny + gy
    up = lax.rem(gy + 1, ny)
    down = lax.rem(gy + ny - 1, ny)

    smalls = [
        pltpu.make_async_copy(source, target, small_sem.at[i])
        for i, (source, target) in enumerate(
            (
                (az_hbm, az_ref),
                (pos_hbm, pos_ref),
                (cross_hbm, cross_ref),
                (lag_hbm, lag_ref),
                (rate_hbm, rate_ref),
                (chord_hbm, chord_ref),
                (twist_hbm, twist_ref),
                (inflow_hbm, inflow_ref),
            )
        )
    ]
    for copy in smalls:
        copy.start()
    slabs = [
        pltpu.make_async_copy(vel_hbm.at[:, :, rows], grid0.at[:, :, rows], load_sem.at[i])
        for i, rows in enumerate((pl.ds(cy - SLAB, SLAB), pl.ds(0, SLAB), pl.ds(SLAB, cy - 2 * SLAB)))
    ]
    for copy in slabs:
        copy.start()

    barrier = pltpu.get_barrier_semaphore()

    for d in range(1, ny):
        pl.semaphore_signal(
            barrier, inc=1, device_id={"gy": lax.rem(gy + d, ny)}, device_id_type=MESH
        )
    for d in range(1, nx):
        pl.semaphore_signal(
            barrier, inc=1, device_id={"gx": lax.rem(gx + d, nx)}, device_id_type=MESH
        )

    for copy in smalls:
        copy.wait()

    rotor, hub_x, load_x, shift_y, valid, az = [], [], [], [], [], []
    for e in range(ENTRIES):
        blade = cross_ref[BLADES * e, tile]
        r = jnp.where(blade >= 0, blade, 0) // BLADES
        rotor.append(jnp.where(blade >= 0, r, -1))
        valid.append(jnp.where(blade >= 0, 1.0, 0.0).astype(f32))
        hub_x.append(jnp.where(blade >= 0, pos_ref[0, r] - gx * cx, 2))
        load_x.append(jnp.clip(hub_x[e], 2, cx - 3))
        off = gy * cy - pos_ref[1, r] + total_y + total_y // 2
        shift_y.append(lax.rem(off, total_y) - total_y // 2)
        az.append(az_ref[r])

    listed = [[cross_ref[BLADES * f, gx * ny + k] for f in range(ENTRIES)] for k in range(ny)]

    def matches(other):
        found = []
        for f in range(ENTRIES):
            blade = cross_ref[BLADES * f, other]
            found.append(jnp.where(blade >= 0, jnp.where(blade >= 0, blade, 0) // BLADES, -2))
        return [
            [jnp.where(rotor[e] == found[f], 1.0, 0.0).astype(f32) for f in range(ENTRIES)]
            for e in range(ENTRIES)
        ]

    row = lax.broadcasted_iota(jnp.int32, (ROWS, nz), 0)
    first = row < BLADES
    lane8 = lax.broadcasted_iota(jnp.int32, (ROWS, nz), 1).astype(f32)
    radius = RADIUS * (lane8 + 0.5) / nz
    spin = jnp.where(first, row, row - BLADES).astype(f32) * (2.0 * math.pi / 3.0)
    base = jnp.where(first, az[0], az[1])
    mask_rows = []
    for other in (gx * ny + down, gx * ny + up):
        m = matches(other)
        mask_rows.append(
            (jnp.where(first, m[0][0], m[1][1]), jnp.where(first, m[0][1], m[1][0]))
        )
    cos_all, sin_all = [], []
    rows_y = lax.broadcasted_iota(jnp.int32, (cy, nz), 0)
    rows_z = lax.broadcasted_iota(jnp.int32, (nz, nz), 0).astype(f32) - HUB
    for n in range(STEPS):
        theta = base + TURN_RATE * n + spin
        cos_n, sin_n = jnp.cos(theta), jnp.sin(theta)
        cos_all.append(cos_n)
        sin_all.append(sin_n)

    def fill_kernels(n):
        rc, rs = radius * cos_all[n], radius * sin_all[n]
        for e in range(ENTRIES):
            y_rel = (rows_y + shift_y[e]).astype(f32)
            for b in range(BLADES):
                i = BLADES * e + b
                kern_y[n, e, :, b * nz : (b + 1) * nz] = taper_kernel(y_rel - rs[i : i + 1]) * valid[e]
                kern_z[n, e, :, b * nz : (b + 1) * nz] = taper_kernel(rows_z - rc[i : i + 1])

    cos_t, sin_t = jnp.cos(twist_ref[...]), jnp.sin(twist_ref[...])
    chord = FORCE_SCALE * chord_ref[...]
    zero_rows = jnp.zeros((ROWS - 2 * BLADES, nz), f32)

    lag_pack[0:BLADES] = lag_ref[...]
    lag_pack[BLADES : 2 * BLADES] = rate_ref[...]
    lag_pack[2 * BLADES : ROWS] = zero_rows

    started = []

    def send(src, dst, send_sem, recv_sem, axis, other):
        copy = pltpu.make_async_remote_copy(
            src_ref=src,
            dst_ref=dst,
            send_sem=send_sem,
            recv_sem=recv_sem,
            device_id={axis: other},
            device_id_type=MESH,
        )
        copy.start()
        started.append(copy)
        return copy

    def send_lag_column():
        copies = [
            send(lag_pack, lag_col.at[gy], ly_send.at[d], ly_recv.at[d], "gy", lax.rem(gy + d, ny))
            for d in range(1, ny)
        ]
        lag_col[gy] = lag_pack[...]
        return copies

    def send_lag_block():
        copies = [
            send(lag_col, lag_in.at[gx], lx_send.at[d], lx_recv.at[d], "gx", lax.rem(gx + d, nx))
            for d in range(1, nx)
        ]
        lag_in[gx] = lag_col[...]
        return copies

    def plane_sum(src, e):
        field = None
        for i in range(-2, 3):
            term = KERN_X[abs(i)] * src[:, load_x[e] + i]
            field = term if field is None else field + term
        return field

    def sample(n, fields):
        sampled = [[], [], []]
        for e in range(ENTRIES):
            inner = jnp.dot(
                fields[e].reshape(3 * cy, nz),
                kern_z[n, e],
                precision=PRECISE,
                preferred_element_type=f32,
            )
            for c in range(3):
                reduced = jnp.sum(inner[c * cy : (c + 1) * cy] * kern_y[n, e], axis=0, keepdims=True)
                sampled[c] += [reduced[:, b * nz : (b + 1) * nz] for b in range(BLADES)]
        s = [jnp.concatenate(sampled[c] + [zero_rows], axis=0) for c in range(3)]
        return s[0], s[1] * cos_all[n] - s[2] * sin_all[n]

    def late_fields():
        fields = []
        for e in range(ENTRIES):
            pair = [pair_x(hub_x[e] - hub_x[f]) for f in range(ENTRIES)]
            low = jnp.where(hub_x[e] == 2, KERN_X[2] * (ADVECT + DIFFUSE), 0.0).astype(f32)
            high = jnp.where(hub_x[e] == cx - 3, KERN_X[2] * DIFFUSE, 0.0).astype(f32)
            planes = []
            for c in range(3):
                rows = []
                for side in range(2):
                    total = None
                    for i in range(-2, 3):
                        term = (DIFFUSE * KERN_X[abs(i)]) * halo_y[side, c, pl.ds(load_x[e] + i, 1), :]
                        total = term if total is None else total + term
                    rows.append(total)
                edge = jnp.where(is_first_y, rows[0], jnp.where(is_last_y, rows[1], 0.0))
                force = pair[0] * spread[0, 0, c] + pair[1] * spread[0, 1, c]
                planes.append((force + edge) + (low * halo_x[0, 0, c] + high * halo_x[0, 1, c]))
            fields.append(jnp.stack(planes))
        return fields

    def faces(n, src):
        flat = src.reshape(3 * cx * cy, nz)
        for c in range(3):
            face_y[n, 0, c] = flat[pl.ds(c * cx * cy + cy - 1, cx, stride=cy), :]
            face_y[n, 1, c] = flat[pl.ds(c * cx * cy, cx, stride=cy), :]

    def send_parts(n):
        copies = [
            send(part_out.at[n], part_in.at[n, gy], ps_send.at[n, d], ps_recv.at[n, d], "gy", lax.rem(gy + d, ny))
            for d in range(1, ny)
        ]
        part_in[n, gy] = part_out[n]
        return copies

    def send_faces(n, target):
        return [
            send(face_y.at[n, 0], target.at[0], hy_send.at[n, 0], hy_recv.at[n, 0], "gy", up),
            send(face_y.at[n, 1], target.at[1], hy_send.at[n, 1], hy_recv.at[n, 1], "gy", down),
        ]

    def x_copies(n, src):
        east = pltpu.make_async_remote_copy(
            src_ref=src.at[:, cx - 1],
            dst_ref=halo_x.at[n, 0],
            send_sem=hx_send.at[n, 0],
            recv_sem=hx_recv.at[n, 0],
            device_id={"gx": lax.rem(gx + 1, nx)},
            device_id_type=MESH,
        )
        west = pltpu.make_async_remote_copy(
            src_ref=src.at[:, 0],
            dst_ref=halo_x.at[n, 1],
            send_sem=hx_send.at[n, 1],
            recv_sem=hx_recv.at[n, 1],
            device_id={"gx": lax.rem(gx + nx - 1, nx)},
            device_id_type=MESH,
        )
        return east, west

    def send_x(n, src):
        east, west = x_copies(n, src)

        @pl.when(gx < nx - 1)
        def _():
            east.start()

        @pl.when(gx > 0)
        def _():
            west.start()

    def wait_x(n, src):
        east, west = x_copies(n, src)

        @pl.when(gx > 0)
        def _():
            east.wait_recv()

        @pl.when(gx == 0)
        def _():
            halo_x[n, 0] = inflow_ref[...]

        @pl.when(gx < nx - 1)
        def _():
            west.wait_recv()

        @pl.when(gx == nx - 1)
        def _():
            halo_x[n, 1] = src[:, cx - 1]

    def wait_x_sent(n, src):
        east, west = x_copies(n, src)

        @pl.when(gx < nx - 1)
        def _():
            east.wait_send()

        @pl.when(gx > 0)
        def _():
            west.wait_send()

    row_c = lax.broadcasted_iota(jnp.int32, (cy, nz), 0)
    is_first_y, is_last_y = row_c == 0, row_c == cy - 1

    def interior(src, dst):
        group = min(GROUP, cx)
        zi = lax.broadcasted_iota(jnp.int32, (2 * nz, nz), 0)
        zi = jnp.where(zi >= nz, zi - nz, zi)
        zo = lax.broadcasted_iota(jnp.int32, (2 * nz, nz), 1)
        near = jnp.where(jnp.abs(zi - zo) == 1, 1.0, 0.0) + jnp.where(zi == zo, CENTRE, 0.0)
        near = near + jnp.where((zi == zo) & (zo == nz - 1), 1.0, 0.0)
        near = near.astype(jnp.bfloat16)

        def planes(k, carry):
            x0 = pl.multiple_of(k * group, group)
            for c in range(3):
                cur = src[c, pl.ds(x0, group)].reshape(group * cy, nz)
                high = cur.astype(jnp.bfloat16)
                low = (cur - high.astype(f32)).astype(jnp.bfloat16)
                z_near = jnp.dot(jnp.concatenate([high, low], axis=1), near, preferred_element_type=f32)
                for g in range(group):
                    x = x0 + g
                    own = src[c, x]
                    y_prev = jnp.where(is_first_y, 0.0, pltpu.roll(own, 1, 0))
                    y_next = jnp.where(is_last_y, 0.0, pltpu.roll(own, cy - 1, 0))
                    total = z_near[g * cy : (g + 1) * cy] + (y_prev + y_next)
                    if g == 0:
                        total = total + jnp.where(x0 > 0, LEAD, 0.0) * src[c, jnp.maximum(x - 1, 0)]
                    else:
                        total = total + LEAD * src[c, x - 1]
                    if g == group - 1:
                        total = total + jnp.where(x0 < cx - group, 1.0, 0.0) * src[c, jnp.minimum(x + 1, cx - 1)]
                    else:
                        total = total + src[c, x + 1]
                    dst[c, x] = DIFFUSE * total
            return carry

        lax.fori_loop(0, cx // group, planes, 0)

    def totals(n):
        whole = []
        for c in range(2):
            total = part_out[n, c]
            for side, other_y in enumerate((down, up)):
                other = part_in[n, other_y, c]
                same, cross = mask_rows[side]
                swapped = jnp.where(first, pltpu.roll(other, ROWS - BLADES, 0), pltpu.roll(other, BLADES, 0))
                total = total + (same * other + cross * swapped)
            whole.append(total)
        return whole

    def relax(lag, rate, axial, turned):
        tangential = SPIN * radius - turned
        magnitude = jnp.sqrt(axial * axial + tangential * tangential + 1.0)
        lift_static = LIFT_SLOPE * (axial * cos_t - tangential * sin_t) / magnitude
        return lag + rate * (lift_static - lag), tangential, magnitude

    def fill_spread(n, lag, axial, tangential, magnitude):
        cos_b, sin_b = cos_all[n], sin_all[n]
        lift = chord * lag * magnitude
        forces = (-lift * tangential, lift * axial * cos_b, -lift * axial * sin_b)
        for e in range(ENTRIES):
            weighted = []
            for c in range(3):
                weighted.append(
                    jnp.concatenate(
                        [
                            forces[c][BLADES * e + b : BLADES * e + b + 1]
                            * kern_y[n, e, :, b * nz : (b + 1) * nz]
                            for b in range(BLADES)
                        ],
                        axis=1,
                    )
                )
            pushed = lax.dot_general(
                jnp.concatenate(weighted, axis=0),
                kern_z[n, e],
                (((1,), (1,)), ((), ())),
                precision=PRECISE,
                preferred_element_type=f32,
            )
            spread[n, e] = pushed.reshape(3, cy, nz)

    def finish(n, dst):
        def body_force(c, x):
            w0, w1 = weight_x(x - hub_x[0]), weight_x(x - hub_x[1])
            return w0 * spread[n, 0, c] + w1 * spread[n, 1, c]

        def halo_rows(c, x):
            ref = (halo_y, late_y)[n]
            return ref[0, c, pl.ds(x, 1), :], ref[1, c, pl.ds(x, 1), :]

        def plane_rest(x, carry):
            for c in range(3):
                below, above = halo_rows(c, x)
                edge = jnp.where(is_first_y, below, jnp.where(is_last_y, above, 0.0))
                dst[c, x] = dst[c, x] + (body_force(c, x) + DIFFUSE * edge)
            return carry

        lax.fori_loop(0, cx, plane_rest, 0, unroll=UNROLL)
        for c in range(3):
            dst[c, 0] = dst[c, 0] + (ADVECT + DIFFUSE) * halo_x[n, 0, c]
            dst[c, cx - 1] = dst[c, cx - 1] + DIFFUSE * halo_x[n, 1, c]

    def send_rows():
        for side, edge in enumerate((cy - 1, 0)):
            for c in range(3):
                for e in range(ENTRIES):
                    rows_out[side, c, e : e + 1] = spread[0, e, c, edge : edge + 1]
                for k in range(2):
                    rows_out[side, c, 2 + k : 3 + k] = halo_x[0, k, c, edge : edge + 1]
        return [
            send(rows_out.at[0], rows_in.at[0], rw_send.at[0], rw_recv.at[0], "gy", up),
            send(rows_out.at[1], rows_in.at[1], rw_send.at[1], rw_recv.at[1], "gy", down),
        ]

    def complete_halo():
        plane_id = lax.broadcasted_iota(jnp.int32, (cx, nz), 0)
        at_low = jnp.where(plane_id == 0, ADVECT + DIFFUSE, 0.0).astype(f32)
        at_high = jnp.where(plane_id == cx - 1, DIFFUSE, 0.0).astype(f32)
        for side, other in enumerate((down, up)):
            weights = []
            for f in range(ENTRIES):
                blade = cross_ref[BLADES * f, gx * ny + other]
                r = jnp.where(blade >= 0, blade, 0) // BLADES
                weights.append(weight_x(plane_id - (pos_ref[0, r] - gx * cx)))
            weights += [at_low, at_high]
            for c in range(3):
                total = late_y[side, c] + DIFFUSE * face_y[0, 1 - side, c]
                for k in range(4):
                    total = total + weights[k] * rows_in[side, c, k : k + 1]
                late_y[side, c] = total

    def home_blocks(n):
        blocks = []
        for k in range(ny):
            axial, turned = part_in[n, k, 0], part_in[n, k, 1]
            blocks.append(jnp.where(first, axial, pltpu.roll(turned, BLADES, 0)))
            blocks.append(jnp.where(first, pltpu.roll(axial, ROWS - BLADES, 0), turned))
        return blocks

    def fill_home(n):
        blocks = home_blocks(n)
        for h in range(nx):
            wanted = BLADES * (h * ny + gy)
            total = None
            for k in range(ny):
                for f in range(ENTRIES):
                    hit = jnp.where(listed[k][f] == wanted, 1.0, 0.0).astype(f32)
                    term = hit * blocks[ENTRIES * k + f]
                    total = term if total is None else total + term
            home_out[h, n] = total

    pl.semaphore_wait(barrier, nx - 1 + ny - 1)
    lags = send_lag_column()
    for copy in slabs[:2]:
        copy.wait()
    faces(0, grid0)
    halos = send_faces(0, halo_y)
    slabs[2].wait()
    send_x(0, grid0)
    fill_kernels(0)
    part_out[0, 0], part_out[0, 1] = sample(0, [plane_sum(grid0, e) for e in range(ENTRIES)])
    parts = send_parts(0)
    interior(grid0, grid1)
    faces(1, grid1)
    for copy in lags:
        copy.wait_recv()
    lags = send_lag_block()
    fill_kernels(1)
    early = sample(1, [plane_sum(grid1, e) for e in range(ENTRIES)])
    for copy in parts:
        copy.wait_recv()
    axial, turned = totals(0)
    for copy in lags:
        copy.wait_recv()
    state_rows, rate_rows = [], []
    for e in range(ENTRIES):
        r = jnp.maximum(rotor[e], 0)
        block = lag_in[r // ny, lax.rem(r, ny)]
        state_rows.append(block[0:BLADES])
        rate_rows.append(block[BLADES : 2 * BLADES])
    lag = jnp.concatenate(state_rows + [zero_rows], axis=0)
    rate = jnp.concatenate(rate_rows + [zero_rows], axis=0)
    lag, tangential, magnitude = relax(lag, rate, axial, turned)
    fill_spread(0, lag, axial, tangential, magnitude)
    wait_x(0, grid0)
    for copy in halos:
        copy.wait_recv()
    late = sample(1, late_fields())
    for c in range(2):
        part_out[1, c] = early[c] + late[c]
    parts = send_parts(1)
    rows = send_rows()
    late_halos = send_faces(1, late_y)
    finish(0, grid1)
    send_x(1, grid1)
    fill_home(0)
    interior(grid1, out_ref)
    for copy in parts:
        copy.wait_recv()
    fill_home(1)
    homes = [
        send(
            home_out.at[lax.rem(gx + d, nx)],
            home_in.at[gx],
            home_send.at[d],
            home_recv.at[d],
            "gx",
            lax.rem(gx + d, nx),
        )
        for d in range(1, nx)
    ]
    home_in[gx] = home_out[gx]
    axial, turned = totals(1)
    lag, tangential, magnitude = relax(lag, rate, axial, turned)
    fill_spread(1, lag, axial, tangential, magnitude)
    wait_x(1, grid1)
    for copy in rows + late_halos:
        copy.wait_recv()
    complete_halo()
    finish(1, out_ref)

    for copy in homes:
        copy.wait_recv()
    own = lag_pack[...]
    state, own_rate = own, pltpu.roll(own, ROWS - BLADES, 0)
    for n in range(STEPS):
        total = home_in[0, n]
        for h in range(1, nx):
            total = total + home_in[h, n]
        state, _, _ = relax(state, own_rate, total, pltpu.roll(total, ROWS - BLADES, 0))
    state_ref[...] = state[0:BLADES]
    for n, src in ((0, grid0), (1, grid1)):
        wait_x_sent(n, src)
    for copy in started:
        copy.wait_send()


def store_kernel(vel_ref, state_ref, vel_hbm, state_hbm, sem):
    width = vel_ref.shape[1] // CHUNKS
    copies = [
        pltpu.make_async_copy(
            vel_ref.at[:, pl.ds(i * width, width)], vel_hbm.at[:, pl.ds(i * width, width)], sem.at[i]
        )
        for i in range(CHUNKS)
    ]
    copies.append(pltpu.make_async_copy(state_ref, state_hbm, sem.at[CHUNKS]))
    for copy in copies:
        copy.start()
    for copy in copies:
        copy.wait()


def per_device(
    velocity, inflow, azimuth, positions, crossings, lag_state, lag_rate, chord_len, twist_angle
):
    nx = lax.axis_size("gx")
    ny = lax.axis_size("gy")
    comps, cx, cy, nz = velocity.shape
    own, sections = lag_state.shape
    assert comps == 3 and own == BLADES and sections == nz
    f32 = jnp.float32
    grid = pltpu.VMEM((3, cx, cy, nz), f32)
    dma = pltpu.SemaphoreType.DMA
    hbm = pl.BlockSpec(memory_space=pltpu.HBM)
    vmem = pl.BlockSpec(memory_space=pltpu.VMEM)
    moved, state = pl.pallas_call(
        functools.partial(farm_kernel, nx, ny),
        out_shape=(pltpu.VMEM(velocity.shape, f32), pltpu.VMEM(lag_state.shape, f32)),
        in_specs=[hbm] * 9,
        out_specs=(vmem, vmem),
        scratch_shapes=[
            pltpu.VMEM(inflow.shape, f32),
            pltpu.SMEM(azimuth.shape, f32),
            pltpu.SMEM(positions.shape[::-1], jnp.int32),
            pltpu.SMEM(crossings.shape[::-1], jnp.int32),
            pltpu.VMEM(lag_state.shape, f32),
            pltpu.VMEM(lag_state.shape, f32),
            pltpu.VMEM((1, sections), f32),
            pltpu.VMEM((1, sections), f32),
            grid,
            grid,
            pltpu.VMEM((STEPS, 2, 3, cy, nz), f32),
            pltpu.VMEM((2, 3, cx, nz), f32),
            pltpu.VMEM((2, 3, cx, nz), f32),
            pltpu.VMEM((STEPS, 2, 3, cx, nz), f32),
            pltpu.VMEM((STEPS, 2, ROWS, nz), f32),
            pltpu.VMEM((STEPS, ny, 2, ROWS, nz), f32),
            pltpu.VMEM((STEPS, ENTRIES, cy, BLADES * nz), f32),
            pltpu.VMEM((STEPS, ENTRIES, nz, BLADES * nz), f32),
            pltpu.VMEM((STEPS, ENTRIES, 3, cy, nz), f32),
            pltpu.VMEM((ROWS, nz), f32),
            pltpu.VMEM((ny, ROWS, nz), f32),
            pltpu.VMEM((nx, ny, ROWS, nz), f32),
            pltpu.VMEM((2, 3, 4, nz), f32),
            pltpu.VMEM((2, 3, 4, nz), f32),
            pltpu.VMEM((nx, STEPS, ROWS, nz), f32),
            pltpu.VMEM((nx, STEPS, ROWS, nz), f32),
            dma((8,)),
            dma((3,)),
            dma((STEPS, 2)),
            dma((STEPS, 2)),
            dma((STEPS, 2)),
            dma((STEPS, 2)),
            dma((STEPS, ny)),
            dma((STEPS, ny)),
            dma((ny,)),
            dma((ny,)),
            dma((nx,)),
            dma((nx,)),
            dma((2,)),
            dma((2,)),
            dma((nx,)),
            dma((nx,)),
        ],
        compiler_params=pltpu.CompilerParams(
            collective_id=0, has_side_effects=True, vmem_limit_bytes=30 * 1024 * 1024
        ),
        cost_estimate=pl.CostEstimate(
            flops=50_000_000, bytes_accessed=8 * velocity.size, transcendentals=500_000
        ),
    )(
        *(
            pltpu.with_memory_space_constraint(source, pltpu.HBM)
            for source in (
                velocity,
                inflow,
                azimuth,
                positions.T,
                crossings.T,
                lag_state,
                lag_rate,
                chord_len.reshape(1, sections),
                twist_angle.reshape(1, sections),
            )
        )
    )
    anywhere = pl.BlockSpec(memory_space=pl.ANY)
    return pl.pallas_call(
        store_kernel,
        out_shape=(
            jax.ShapeDtypeStruct(velocity.shape, f32),
            jax.ShapeDtypeStruct(lag_state.shape, f32),
        ),
        in_specs=[anywhere] * 2,
        out_specs=(pl.BlockSpec(memory_space=pltpu.HBM),) * 2,
        scratch_shapes=[dma((CHUNKS + 1,))],
        compiler_params=pltpu.CompilerParams(vmem_limit_bytes=16 * 1024 * 1024),
    )(
        pltpu.with_memory_space_constraint(moved, pltpu.VMEM),
        pltpu.with_memory_space_constraint(state, pltpu.VMEM),
    )


def solution(mesh):
    return jax.shard_map(
        per_device,
        mesh=mesh,
        in_specs=(
            P(None, "gx", "gy", None),
            P(None, "gy", None),
            P(),
            P(),
            P(),
            P(("gx", "gy"), None),
            P(("gx", "gy"), None),
            P(),
            P(),
        ),
        out_specs=(P(None, "gx", "gy", None), P(("gx", "gy"), None)),
        check_vma=False,
    )
```

```python
import functools
import math

import jax
import jax.numpy as jnp
from jax import lax
from jax.experimental import pallas as pl
from jax.experimental.pallas import tpu as pltpu
from jax.sharding import PartitionSpec as P

RADIUS = 12
HUB = 15
STEPS = 2
EPSILON = 2.0
SUPPORT = 3.0
TURN_RATE = 0.1
SPIN = 0.25
LIFT_SLOPE = 2.0 * math.pi
FORCE_SCALE = 0.15
ADVECT = 0.5
DIFFUSE = 0.05
PRECISE = lax.Precision.HIGH
MESH = pl.DeviceIdType.MESH
CENTRE = round((1.0 - ADVECT - 6.0 * DIFFUSE) / DIFFUSE)
LEAD = (ADVECT + DIFFUSE) / DIFFUSE
GROUP = 16
BLADES = 3
ENTRIES = 2
ROWS = 8
UNROLL = 4
SLAB = 8
CHUNKS = 4


def taper_const(distance):
    square = distance * distance
    term = max(1.0 - square / (SUPPORT * SUPPORT), 0.0)
    return math.exp(-square / EPSILON**2) * term * term / (EPSILON * math.sqrt(math.pi))


KERN_X = [taper_const(float(i)) for i in range(3)]
PAIR_X = [
    sum(KERN_X[abs(i)] * KERN_X[abs(i + d)] for i in range(-2, 3) if abs(i + d) <= 2) for d in range(5)
]


def taper_kernel(distance):
    square = distance * distance
    term = jnp.maximum(1.0 - square * (1.0 / (SUPPORT * SUPPORT)), 0.0)
    return (
        jnp.exp(square * (-1.0 / (EPSILON * EPSILON)))
        * (term * term)
        * (1.0 / (EPSILON * math.sqrt(math.pi)))
    )


def weight_x(offset):
    dist = jnp.abs(offset)
    return jnp.where(
        dist == 0,
        KERN_X[0],
        jnp.where(dist == 1, KERN_X[1], jnp.where(dist == 2, KERN_X[2], 0.0)),
    ).astype(jnp.float32)


def pair_x(offset):
    dist = jnp.abs(offset)
    total = jnp.where(dist == 0, PAIR_X[0], 0.0)
    for d in range(1, 5):
        total = jnp.where(dist == d, PAIR_X[d], total)
    return total.astype(jnp.float32)


def farm_kernel(
    nx,
    ny,
    vel_hbm,
    inflow_hbm,
    az_hbm,
    pos_hbm,
    cross_hbm,
    lag_hbm,
    rate_hbm,
    chord_hbm,
    twist_hbm,
    out_ref,
    state_ref,
    inflow_ref,
    az_ref,
    pos_ref,
    cross_ref,
    lag_ref,
    rate_ref,
    chord_ref,
    twist_ref,
    grid0,
    grid1,
    halo_x,
    halo_y,
    late_y,
    face_y,
    part_out,
    part_in,
    kern_y,
    kern_z,
    spread,
    lag_pack,
    lag_col,
    lag_out,
    lag_in,
    rows_out,
    rows_in,
    edge_out,
    edge_in,
    home_out,
    home_in,
    small_sem,
    load_sem,
    hx_send,
    hx_recv,
    hy_send,
    hy_recv,
    ps_send,
    ps_recv,
    ly_send,
    ly_recv,
    lx_send,
    lx_recv,
    rw_send,
    rw_recv,
    ed_send,
    ed_recv,
    home_send,
    home_recv,
):
    f32 = jnp.float32
    _, cx, cy, nz = grid0.shape
    total_y = cy * ny
    gx = lax.axis_index("gx")
    gy = lax.axis_index("gy")
    tile = gx * ny + gy
    up = lax.rem(gy + 1, ny)
    down = lax.rem(gy + ny - 1, ny)

    smalls = [
        pltpu.make_async_copy(source, target, small_sem.at[i])
        for i, (source, target) in enumerate(
            (
                (lag_hbm, lag_ref),
                (rate_hbm, rate_ref),
                (az_hbm, az_ref),
                (pos_hbm, pos_ref),
                (cross_hbm, cross_ref),
                (chord_hbm, chord_ref),
                (twist_hbm, twist_ref),
                (inflow_hbm, inflow_ref),
            )
        )
    ]
    for copy in smalls:
        copy.start()
    slabs = [
        pltpu.make_async_copy(vel_hbm.at[:, :, rows], grid0.at[:, :, rows], load_sem.at[i])
        for i, rows in enumerate((pl.ds(cy - SLAB, SLAB), pl.ds(0, SLAB), pl.ds(SLAB, cy - 2 * SLAB)))
    ]
    for copy in slabs:
        copy.start()

    barrier = pltpu.get_barrier_semaphore()

    for d in range(1, ny):
        pl.semaphore_signal(
            barrier, inc=1, device_id={"gy": lax.rem(gy + d, ny)}, device_id_type=MESH
        )
    for d in range(1, nx):
        pl.semaphore_signal(
            barrier, inc=1, device_id={"gx": lax.rem(gx + d, nx)}, device_id_type=MESH
        )

    for copy in smalls[:2]:
        copy.wait()
    zero_rows = jnp.zeros((ROWS - 2 * BLADES, nz), f32)
    lag_pack[0:BLADES] = lag_ref[...]
    lag_pack[BLADES : 2 * BLADES] = rate_ref[...]
    lag_pack[2 * BLADES : ROWS] = zero_rows
    started = []

    def send(src, dst, send_sem, recv_sem, axis, other):
        copy = pltpu.make_async_remote_copy(
            src_ref=src,
            dst_ref=dst,
            send_sem=send_sem,
            recv_sem=recv_sem,
            device_id={axis: other},
            device_id_type=MESH,
        )
        copy.start()
        started.append(copy)
        return copy

    def send_lag_column():
        copies = [
            send(lag_pack, lag_col.at[gy], ly_send.at[d], ly_recv.at[d], "gy", lax.rem(gy + d, ny))
            for d in range(1, ny)
        ]
        lag_col[gy] = lag_pack[...]
        return copies

    pl.semaphore_wait(barrier, nx - 1 + ny - 1)
    lags = send_lag_column()
    for copy in smalls[2:]:
        copy.wait()

    rotor, hub_x, load_x, shift_y, valid, az = [], [], [], [], [], []
    for e in range(ENTRIES):
        blade = cross_ref[BLADES * e, tile]
        r = jnp.where(blade >= 0, blade, 0) // BLADES
        rotor.append(jnp.where(blade >= 0, r, -1))
        valid.append(jnp.where(blade >= 0, 1.0, 0.0).astype(f32))
        hub_x.append(jnp.where(blade >= 0, pos_ref[0, r] - gx * cx, 2))
        load_x.append(jnp.clip(hub_x[e], 2, cx - 3))
        off = gy * cy - pos_ref[1, r] + total_y + total_y // 2
        shift_y.append(lax.rem(off, total_y) - total_y // 2)
        az.append(az_ref[r])

    listed = [[cross_ref[BLADES * f, gx * ny + k] for f in range(ENTRIES)] for k in range(ny)]

    def matches(other):
        found = []
        for f in range(ENTRIES):
            blade = cross_ref[BLADES * f, other]
            found.append(jnp.where(blade >= 0, jnp.where(blade >= 0, blade, 0) // BLADES, -2))
        return [
            [jnp.where(rotor[e] == found[f], 1.0, 0.0).astype(f32) for f in range(ENTRIES)]
            for e in range(ENTRIES)
        ]

    row = lax.broadcasted_iota(jnp.int32, (ROWS, nz), 0)
    first = row < BLADES
    lane8 = lax.broadcasted_iota(jnp.int32, (ROWS, nz), 1).astype(f32)
    radius = RADIUS * (lane8 + 0.5) / nz
    spin = jnp.where(first, row, row - BLADES).astype(f32) * (2.0 * math.pi / 3.0)
    base = jnp.where(first, az[0], az[1])
    mask_rows = []
    for other in (gx * ny + down, gx * ny + up):
        m = matches(other)
        mask_rows.append(
            (jnp.where(first, m[0][0], m[1][1]), jnp.where(first, m[0][1], m[1][0]))
        )
    cos_all, sin_all = [], []
    rows_y = lax.broadcasted_iota(jnp.int32, (cy, nz), 0)
    rows_z = lax.broadcasted_iota(jnp.int32, (nz, nz), 0).astype(f32) - HUB
    for n in range(STEPS):
        theta = base + TURN_RATE * n + spin
        cos_n, sin_n = jnp.cos(theta), jnp.sin(theta)
        cos_all.append(cos_n)
        sin_all.append(sin_n)

    def fill_kernels(n):
        rc, rs = radius * cos_all[n], radius * sin_all[n]
        for e in range(ENTRIES):
            y_rel = (rows_y + shift_y[e]).astype(f32)
            for b in range(BLADES):
                i = BLADES * e + b
                kern_y[n, e, :, b * nz : (b + 1) * nz] = taper_kernel(y_rel - rs[i : i + 1]) * valid[e]
                kern_z[n, e, :, b * nz : (b + 1) * nz] = taper_kernel(rows_z - rc[i : i + 1])

    cos_t, sin_t = jnp.cos(twist_ref[...]), jnp.sin(twist_ref[...])
    chord = FORCE_SCALE * chord_ref[...]


    def send_lag_block():
        for h in range(nx):
            for f in range(ENTRIES):
                blade = cross_ref[BLADES * f, h * ny + gy]
                r = jnp.where(blade >= 0, blade, 0) // BLADES
                lag_out[h, f] = lag_col[lax.rem(r, ny)]
        copies = []
        for d in range(1, nx):
            other = lax.rem(gx + d, nx)
            copies.append(send(lag_out.at[other], lag_in.at[gx], lx_send.at[d], lx_recv.at[d], "gx", other))
        lag_in[gx] = lag_out[gx]
        return copies

    def plane_sum(src, e):
        field = None
        for i in range(-2, 3):
            term = KERN_X[abs(i)] * src[:, load_x[e] + i]
            field = term if field is None else field + term
        return field

    def sample(n, fields):
        sampled = [[], [], []]
        for e in range(ENTRIES):
            inner = jnp.dot(
                fields[e].reshape(3 * cy, nz),
                kern_z[n, e],
                precision=PRECISE,
                preferred_element_type=f32,
            )
            for c in range(3):
                reduced = jnp.sum(inner[c * cy : (c + 1) * cy] * kern_y[n, e], axis=0, keepdims=True)
                sampled[c] += [reduced[:, b * nz : (b + 1) * nz] for b in range(BLADES)]
        s = [jnp.concatenate(sampled[c] + [zero_rows], axis=0) for c in range(3)]
        return s[0], s[1] * cos_all[n] - s[2] * sin_all[n]

    def late_fields():
        fields = []
        for e in range(ENTRIES):
            pair = [pair_x(hub_x[e] - hub_x[f]) for f in range(ENTRIES)]
            low = jnp.where(hub_x[e] == 2, KERN_X[2] * (ADVECT + DIFFUSE), 0.0).astype(f32)
            high = jnp.where(hub_x[e] == cx - 3, KERN_X[2] * DIFFUSE, 0.0).astype(f32)
            planes = []
            for c in range(3):
                k = 3 * e + c
                rows = [edge_in[side, k : k + 1] for side in range(2)]
                edge = jnp.where(is_first_y, rows[0], jnp.where(is_last_y, rows[1], 0.0))
                force = pair[0] * spread[0, 0, c] + pair[1] * spread[0, 1, c]
                planes.append((force + edge) + (low * halo_x[0, 0, c] + high * halo_x[0, 1, c]))
            fields.append(jnp.stack(planes))
        return fields

    def faces(n, src):
        flat = src.reshape(3 * cx * cy, nz)
        for c in range(3):
            face_y[n, 0, c] = flat[pl.ds(c * cx * cy + cy - 1, cx, stride=cy), :]
            face_y[n, 1, c] = flat[pl.ds(c * cx * cy, cx, stride=cy), :]

    def send_parts(n):
        copies = [
            send(part_out.at[n], part_in.at[n, gy], ps_send.at[n, d], ps_recv.at[n, d], "gy", lax.rem(gy + d, ny))
            for d in range(1, ny)
        ]
        part_in[n, gy] = part_out[n]
        return copies

    def send_faces(n, target):
        return [
            send(face_y.at[n, 0], target.at[0], hy_send.at[n, 0], hy_recv.at[n, 0], "gy", up),
            send(face_y.at[n, 1], target.at[1], hy_send.at[n, 1], hy_recv.at[n, 1], "gy", down),
        ]

    def send_edges():
        for side, other in enumerate((up, down)):
            for f in range(ENTRIES):
                blade = cross_ref[BLADES * f, gx * ny + other]
                r = jnp.where(blade >= 0, blade, 0) // BLADES
                centre = jnp.where(blade >= 0, jnp.clip(pos_ref[0, r] - gx * cx, 2, cx - 3), 2)
                for c in range(3):
                    total = None
                    for i in range(-2, 3):
                        term = (DIFFUSE * KERN_X[abs(i)]) * face_y[0, side, c, pl.ds(centre + i, 1), :]
                        total = term if total is None else total + term
                    k = 3 * f + c
                    edge_out[side, k : k + 1] = total
            edge_out[side, 3 * ENTRIES : ROWS] = zero_rows
        return [
            send(edge_out.at[0], edge_in.at[0], ed_send.at[0], ed_recv.at[0], "gy", up),
            send(edge_out.at[1], edge_in.at[1], ed_send.at[1], ed_recv.at[1], "gy", down),
        ]

    def x_copies(n, src):
        east = pltpu.make_async_remote_copy(
            src_ref=src.at[:, cx - 1],
            dst_ref=halo_x.at[n, 0],
            send_sem=hx_send.at[n, 0],
            recv_sem=hx_recv.at[n, 0],
            device_id={"gx": lax.rem(gx + 1, nx)},
            device_id_type=MESH,
        )
        west = pltpu.make_async_remote_copy(
            src_ref=src.at[:, 0],
            dst_ref=halo_x.at[n, 1],
            send_sem=hx_send.at[n, 1],
            recv_sem=hx_recv.at[n, 1],
            device_id={"gx": lax.rem(gx + nx - 1, nx)},
            device_id_type=MESH,
        )
        return east, west

    def send_x(n, src):
        east, west = x_copies(n, src)

        @pl.when(gx < nx - 1)
        def _():
            east.start()

        @pl.when(gx > 0)
        def _():
            west.start()

    def wait_x(n, src):
        east, west = x_copies(n, src)

        @pl.when(gx > 0)
        def _():
            east.wait_recv()

        @pl.when(gx == 0)
        def _():
            halo_x[n, 0] = inflow_ref[...]

        @pl.when(gx < nx - 1)
        def _():
            west.wait_recv()

        @pl.when(gx == nx - 1)
        def _():
            halo_x[n, 1] = src[:, cx - 1]

    def wait_x_sent(n, src):
        east, west = x_copies(n, src)

        @pl.when(gx < nx - 1)
        def _():
            east.wait_send()

        @pl.when(gx > 0)
        def _():
            west.wait_send()

    row_c = lax.broadcasted_iota(jnp.int32, (cy, nz), 0)
    is_first_y, is_last_y = row_c == 0, row_c == cy - 1

    def interior(src, dst):
        group = min(GROUP, cx)
        zi = lax.broadcasted_iota(jnp.int32, (2 * nz, nz), 0)
        zi = jnp.where(zi >= nz, zi - nz, zi)
        zo = lax.broadcasted_iota(jnp.int32, (2 * nz, nz), 1)
        near = jnp.where(jnp.abs(zi - zo) == 1, 1.0, 0.0) + jnp.where(zi == zo, CENTRE, 0.0)
        near = near + jnp.where((zi == zo) & (zo == nz - 1), 1.0, 0.0)
        near = near.astype(jnp.bfloat16)

        def planes(k, carry):
            x0 = pl.multiple_of(k * group, group)
            for c in range(3):
                cur = src[c, pl.ds(x0, group)].reshape(group * cy, nz)
                high = cur.astype(jnp.bfloat16)
                low = (cur - high.astype(f32)).astype(jnp.bfloat16)
                z_near = jnp.dot(jnp.concatenate([high, low], axis=1), near, preferred_element_type=f32)
                for g in range(group):
                    x = x0 + g
                    own = src[c, x]
                    y_prev = jnp.where(is_first_y, 0.0, pltpu.roll(own, 1, 0))
                    y_next = jnp.where(is_last_y, 0.0, pltpu.roll(own, cy - 1, 0))
                    total = z_near[g * cy : (g + 1) * cy] + (y_prev + y_next)
                    if g == 0:
                        total = total + jnp.where(x0 > 0, LEAD, 0.0) * src[c, jnp.maximum(x - 1, 0)]
                    else:
                        total = total + LEAD * src[c, x - 1]
                    if g == group - 1:
                        total = total + jnp.where(x0 < cx - group, 1.0, 0.0) * src[c, jnp.minimum(x + 1, cx - 1)]
                    else:
                        total = total + src[c, x + 1]
                    dst[c, x] = DIFFUSE * total
            return carry

        lax.fori_loop(0, cx // group, planes, 0)

    def totals(n):
        whole = []
        for c in range(2):
            total = part_out[n, c]
            for side, other_y in enumerate((down, up)):
                other = part_in[n, other_y, c]
                same, cross = mask_rows[side]
                swapped = jnp.where(first, pltpu.roll(other, ROWS - BLADES, 0), pltpu.roll(other, BLADES, 0))
                total = total + (same * other + cross * swapped)
            whole.append(total)
        return whole

    def relax(lag, rate, axial, turned):
        tangential = SPIN * radius - turned
        magnitude = jnp.sqrt(axial * axial + tangential * tangential + 1.0)
        lift_static = LIFT_SLOPE * (axial * cos_t - tangential * sin_t) / magnitude
        return lag + rate * (lift_static - lag), tangential, magnitude

    def fill_spread(n, lag, axial, tangential, magnitude):
        cos_b, sin_b = cos_all[n], sin_all[n]
        lift = chord * lag * magnitude
        forces = (-lift * tangential, lift * axial * cos_b, -lift * axial * sin_b)
        for e in range(ENTRIES):
            weighted = []
            for c in range(3):
                weighted.append(
                    jnp.concatenate(
                        [
                            forces[c][BLADES * e + b : BLADES * e + b + 1]
                            * kern_y[n, e, :, b * nz : (b + 1) * nz]
                            for b in range(BLADES)
                        ],
                        axis=1,
                    )
                )
            pushed = lax.dot_general(
                jnp.concatenate(weighted, axis=0),
                kern_z[n, e],
                (((1,), (1,)), ((), ())),
                precision=PRECISE,
                preferred_element_type=f32,
            )
            spread[n, e] = pushed.reshape(3, cy, nz)

    def push(n, dst):
        def plane(x, carry):
            w0, w1 = weight_x(x - hub_x[0]), weight_x(x - hub_x[1])
            for c in range(3):
                dst[c, x] = dst[c, x] + (w0 * spread[n, 0, c] + w1 * spread[n, 1, c])
            return carry

        lax.fori_loop(0, cx, plane, 0, unroll=UNROLL)

    def add_x(n, dst):
        for c in range(3):
            dst[c, 0] = dst[c, 0] + (ADVECT + DIFFUSE) * halo_x[n, 0, c]
            dst[c, cx - 1] = dst[c, cx - 1] + DIFFUSE * halo_x[n, 1, c]

    row_s = lax.broadcasted_iota(jnp.int32, (SLAB, nz), 0)
    is_low, is_high = row_s == 0, row_s == SLAB - 1

    def add_y(n, dst):
        def plane(x, carry):
            at = pl.ds(x, 1)
            for c in range(3):
                below, above = halo_y[0, c, at, :], halo_y[1, c, at, :]
                if n == 1:
                    below, above = below + late_y[0, c, at, :], above + late_y[1, c, at, :]
                low, high = pl.ds(0, SLAB), pl.ds(cy - SLAB, SLAB)
                dst[c, x, low] = dst[c, x, low] + jnp.where(is_low, DIFFUSE * below, 0.0)
                dst[c, x, high] = dst[c, x, high] + jnp.where(is_high, DIFFUSE * above, 0.0)
            return carry

        lax.fori_loop(0, cx, plane, 0, unroll=2 * UNROLL)

    def send_rows():
        for side, edge in enumerate((cy - 1, 0)):
            for c in range(3):
                for e in range(ENTRIES):
                    rows_out[side, c, e : e + 1] = spread[0, e, c, edge : edge + 1]
                for k in range(2):
                    rows_out[side, c, 2 + k : 3 + k] = halo_x[0, k, c, edge : edge + 1]
        return [
            send(rows_out.at[0], rows_in.at[0], rw_send.at[0], rw_recv.at[0], "gy", up),
            send(rows_out.at[1], rows_in.at[1], rw_send.at[1], rw_recv.at[1], "gy", down),
        ]

    def complete_halo():
        plane_id = lax.broadcasted_iota(jnp.int32, (cx, nz), 0)
        at_low = jnp.where(plane_id == 0, ADVECT + DIFFUSE, 0.0).astype(f32)
        at_high = jnp.where(plane_id == cx - 1, DIFFUSE, 0.0).astype(f32)
        for side, other in enumerate((down, up)):
            weights = []
            for f in range(ENTRIES):
                blade = cross_ref[BLADES * f, gx * ny + other]
                r = jnp.where(blade >= 0, blade, 0) // BLADES
                weights.append(weight_x(plane_id - (pos_ref[0, r] - gx * cx)))
            weights += [at_low, at_high]
            for c in range(3):
                total = DIFFUSE * face_y[0, 1 - side, c]
                for k in range(4):
                    total = total + weights[k] * rows_in[side, c, k : k + 1]
                halo_y[side, c] = total

    def home_blocks(n):
        blocks = []
        for k in range(ny):
            axial, turned = part_in[n, k, 0], part_in[n, k, 1]
            blocks.append(jnp.where(first, axial, pltpu.roll(turned, BLADES, 0)))
            blocks.append(jnp.where(first, pltpu.roll(axial, ROWS - BLADES, 0), turned))
        return blocks

    def fill_home(n):
        blocks = home_blocks(n)
        for h in range(nx):
            wanted = BLADES * (h * ny + gy)
            total = None
            for k in range(ny):
                for f in range(ENTRIES):
                    hit = jnp.where(listed[k][f] == wanted, 1.0, 0.0).astype(f32)
                    term = hit * blocks[ENTRIES * k + f]
                    total = term if total is None else total + term
            home_out[h, n] = total

    fill_kernels(0)
    for copy in slabs:
        copy.wait()
    part_out[0, 0], part_out[0, 1] = sample(0, [plane_sum(grid0, e) for e in range(ENTRIES)])
    parts = send_parts(0)
    faces(0, grid0)
    edges = send_edges()
    halos = send_faces(0, halo_y)
    send_x(0, grid0)
    interior(grid0, grid1)
    faces(1, grid1)
    for copy in lags:
        copy.wait_recv()
    lags = send_lag_block()
    fill_kernels(1)
    early = sample(1, [plane_sum(grid1, e) for e in range(ENTRIES)])
    for copy in parts:
        copy.wait_recv()
    axial, turned = totals(0)
    for copy in lags:
        copy.wait_recv()
    state_rows, rate_rows = [], []
    for e in range(ENTRIES):
        r = jnp.maximum(rotor[e], 0)
        block = lag_in[r // ny, e]
        state_rows.append(block[0:BLADES])
        rate_rows.append(block[BLADES : 2 * BLADES])
    lag = jnp.concatenate(state_rows + [zero_rows], axis=0)
    rate = jnp.concatenate(rate_rows + [zero_rows], axis=0)
    lag, tangential, magnitude = relax(lag, rate, axial, turned)
    fill_spread(0, lag, axial, tangential, magnitude)
    wait_x(0, grid0)
    for copy in edges:
        copy.wait_recv()
    late = sample(1, late_fields())
    for c in range(2):
        part_out[1, c] = early[c] + late[c]
    parts = send_parts(1)
    rows = send_rows()
    late_halos = send_faces(1, late_y)
    for copy in halos:
        copy.wait_recv()
    push(0, grid1)
    add_x(0, grid1)
    add_y(0, grid1)
    send_x(1, grid1)
    fill_home(0)
    interior(grid1, out_ref)
    for copy in parts:
        copy.wait_recv()
    fill_home(1)
    homes = [
        send(
            home_out.at[lax.rem(gx + d, nx)],
            home_in.at[gx],
            home_send.at[d],
            home_recv.at[d],
            "gx",
            lax.rem(gx + d, nx),
        )
        for d in range(1, nx)
    ]
    home_in[gx] = home_out[gx]
    axial, turned = totals(1)
    lag, tangential, magnitude = relax(lag, rate, axial, turned)
    fill_spread(1, lag, axial, tangential, magnitude)
    push(1, out_ref)
    for copy in rows:
        copy.wait_recv()
    complete_halo()
    wait_x(1, grid1)
    add_x(1, out_ref)
    for copy in late_halos:
        copy.wait_recv()
    add_y(1, out_ref)

    for copy in homes:
        copy.wait_recv()
    own = lag_pack[...]
    state, own_rate = own, pltpu.roll(own, ROWS - BLADES, 0)
    for n in range(STEPS):
        total = home_in[0, n]
        for h in range(1, nx):
            total = total + home_in[h, n]
        state, _, _ = relax(state, own_rate, total, pltpu.roll(total, ROWS - BLADES, 0))
    state_ref[...] = state[0:BLADES]
    for n, src in ((0, grid0), (1, grid1)):
        wait_x_sent(n, src)
    for copy in started:
        copy.wait_send()


def store_kernel(vel_ref, state_ref, vel_hbm, state_hbm, sem):
    width = vel_ref.shape[1] // CHUNKS
    copies = [
        pltpu.make_async_copy(
            vel_ref.at[:, pl.ds(i * width, width)], vel_hbm.at[:, pl.ds(i * width, width)], sem.at[i]
        )
        for i in range(CHUNKS)
    ]
    copies.append(pltpu.make_async_copy(state_ref, state_hbm, sem.at[CHUNKS]))
    for copy in copies:
        copy.start()
    for copy in copies:
        copy.wait()


def per_device(
    velocity, inflow, azimuth, positions, crossings, lag_state, lag_rate, chord_len, twist_angle
):
    nx = lax.axis_size("gx")
    ny = lax.axis_size("gy")
    comps, cx, cy, nz = velocity.shape
    own, sections = lag_state.shape
    assert comps == 3 and own == BLADES and sections == nz
    f32 = jnp.float32
    grid = pltpu.VMEM((3, cx, cy, nz), f32)
    dma = pltpu.SemaphoreType.DMA
    hbm = pl.BlockSpec(memory_space=pltpu.HBM)
    vmem = pl.BlockSpec(memory_space=pltpu.VMEM)
    moved, state = pl.pallas_call(
        functools.partial(farm_kernel, nx, ny),
        out_shape=(pltpu.VMEM(velocity.shape, f32), pltpu.VMEM(lag_state.shape, f32)),
        in_specs=[hbm] * 9,
        out_specs=(vmem, vmem),
        scratch_shapes=[
            pltpu.VMEM(inflow.shape, f32),
            pltpu.SMEM(azimuth.shape, f32),
            pltpu.SMEM(positions.shape[::-1], jnp.int32),
            pltpu.SMEM(crossings.shape[::-1], jnp.int32),
            pltpu.VMEM(lag_state.shape, f32),
            pltpu.VMEM(lag_state.shape, f32),
            pltpu.VMEM((1, sections), f32),
            pltpu.VMEM((1, sections), f32),
            grid,
            grid,
            pltpu.VMEM((STEPS, 2, 3, cy, nz), f32),
            pltpu.VMEM((2, 3, cx, nz), f32),
            pltpu.VMEM((2, 3, cx, nz), f32),
            pltpu.VMEM((STEPS, 2, 3, cx, nz), f32),
            pltpu.VMEM((STEPS, 2, ROWS, nz), f32),
            pltpu.VMEM((STEPS, ny, 2, ROWS, nz), f32),
            pltpu.VMEM((STEPS, ENTRIES, cy, BLADES * nz), f32),
            pltpu.VMEM((STEPS, ENTRIES, nz, BLADES * nz), f32),
            pltpu.VMEM((STEPS, ENTRIES, 3, cy, nz), f32),
            pltpu.VMEM((ROWS, nz), f32),
            pltpu.VMEM((ny, ROWS, nz), f32),
            pltpu.VMEM((nx, ENTRIES, ROWS, nz), f32),
            pltpu.VMEM((nx, ENTRIES, ROWS, nz), f32),
            pltpu.VMEM((2, 3, 4, nz), f32),
            pltpu.VMEM((2, 3, 4, nz), f32),
            pltpu.VMEM((2, ROWS, nz), f32),
            pltpu.VMEM((2, ROWS, nz), f32),
            pltpu.VMEM((nx, STEPS, ROWS, nz), f32),
            pltpu.VMEM((nx, STEPS, ROWS, nz), f32),
            dma((8,)),
            dma((3,)),
            dma((STEPS, 2)),
            dma((STEPS, 2)),
            dma((STEPS, 2)),
            dma((STEPS, 2)),
            dma((STEPS, ny)),
            dma((STEPS, ny)),
            dma((ny,)),
            dma((ny,)),
            dma((nx,)),
            dma((nx,)),
            dma((2,)),
            dma((2,)),
            dma((2,)),
            dma((2,)),
            dma((nx,)),
            dma((nx,)),
        ],
        compiler_params=pltpu.CompilerParams(
            collective_id=0, has_side_effects=True, vmem_limit_bytes=30 * 1024 * 1024
        ),
        cost_estimate=pl.CostEstimate(
            flops=50_000_000, bytes_accessed=8 * velocity.size, transcendentals=500_000
        ),
    )(
        *(
            pltpu.with_memory_space_constraint(source, pltpu.HBM)
            for source in (
                velocity,
                inflow,
                azimuth,
                positions.T,
                crossings.T,
                lag_state,
                lag_rate,
                chord_len.reshape(1, sections),
                twist_angle.reshape(1, sections),
            )
        )
    )
    anywhere = pl.BlockSpec(memory_space=pl.ANY)
    return pl.pallas_call(
        store_kernel,
        out_shape=(
            jax.ShapeDtypeStruct(velocity.shape, f32),
            jax.ShapeDtypeStruct(lag_state.shape, f32),
        ),
        in_specs=[anywhere] * 2,
        out_specs=(pl.BlockSpec(memory_space=pltpu.HBM),) * 2,
        scratch_shapes=[dma((CHUNKS + 1,))],
        compiler_params=pltpu.CompilerParams(vmem_limit_bytes=16 * 1024 * 1024),
    )(
        pltpu.with_memory_space_constraint(moved, pltpu.VMEM),
        pltpu.with_memory_space_constraint(state, pltpu.VMEM),
    )


def solution(mesh):
    return jax.shard_map(
        per_device,
        mesh=mesh,
        in_specs=(
            P(None, "gx", "gy", None),
            P(None, "gy", None),
            P(),
            P(),
            P(),
            P(("gx", "gy"), None),
            P(("gx", "gy"), None),
            P(),
            P(),
        ),
        out_specs=(P(None, "gx", "gy", None), P(("gx", "gy"), None)),
        check_vma=False,
    )
```
